256 devices in a mesh: row: 16 (over x, y), col: 16 (over z, core).
Axes of the slice: x: 4, y: 4, z: 8, core: 2. Of those that a mesh axis runs over, the one named last changes fastest.
Arguments:
- pan_left: bfloat16 [2, 16, 2048, 64], P(None, 'row', 'col')
- pan_right: bfloat16 [2, 16, 2048, 64], P(None, 'row', 'col')
- panel_rank: int32 [2, 16], P(None, 'row'), may hold values from 8 to 64, as said below
- diag_tiles: float32 [2, 16, 2048, 2048], P(None, 'row', 'col'), as said below
- col_right: bfloat16 [2, 16, 64, 2048], P(None, 'row', 'col'), may hold values from -6 to 6
- column_rank: int32 [2, 16], P(None, 'row'), may hold values from 8 to 64, as said below
Outputs:
- panel_update: bfloat16 [2, 16, 2, 16, 2048, 64], P(None, 'row', None, 'col')
- diag_new: float32 [2, 16, 2048, 2048], P(None, 'row', 'col')
- lead_factor: float32 [2048, 2048], P('row', 'col')
- col_solved: float32 [2, 16, 64, 2048], P(None, 'row', 'col')
The draws below stay inside these ranges and needn't reach their ends.
Inputs may be any that keep to these rules, and one draw needn't show every extreme that they name: `panel_rank`: some tile has rank exactly 8 and some exactly 64. `column_rank`: some tile has rank exactly 8 and some exactly 64. `diag_tiles`: every tile is symmetric and diag_new for tile 0 is positive definite.
All inputs are finite; a program needn't handle non-finite values.
Results may differ from the reference program's by a relative error of at most 0.0049.
Values may be sent and summed in bfloat16 or wider, within the bound.
A program may use at most 128 MiB of HBM per device.

```python
import jax
import jax.numpy as jnp
from jax import lax

NB = 2048
R = 64
TPR = 2
TPC = 2
N_ROW = 16
N_COL = 16


def rank_draw(key):
    first, second = jax.random.split(key)
    tile_count = TPR * N_ROW
    ranks = jax.random.randint(first, (tile_count,), 8, R + 1)
    picks = jax.random.permutation(second, tile_count)
    ranks = ranks.at[picks[0]].set(R).at[picks[1]].set(8)
    return ranks.reshape(TPR, N_ROW).astype(jnp.int32)


def panel_draw(key):
    first, second, third = jax.random.split(key, 3)
    right_scale = 3.0
    left_scale = 2.0 / (3.0 * NB)
    left_factor = jnp.clip(jax.random.normal(first, (TPR, N_ROW, NB, R), jnp.float32), -6.0, 6.0) * left_scale
    right_factor = jnp.clip(jax.random.normal(second, (TPR, N_ROW, NB, R), jnp.float32), -6.0, 6.0) * right_scale
    return (left_factor, right_factor, rank_draw(third))


def draw_pan_left(key, part):
    left_factor, right_factor, ranks = panel_draw(key)
    return left_factor.astype(jnp.bfloat16)


def draw_pan_right(key, part):
    left_factor, right_factor, ranks = panel_draw(key)
    return right_factor.astype(jnp.bfloat16)


def draw_panel_rank(key, part):
    left_factor, right_factor, ranks = panel_draw(key)
    return ranks


def matern_base(key, length, scale_lo, scale_hi):
    jitter_key, scale_key, noise_key, nugget_key = jax.random.split(key, 4)
    cell_ids = lax.broadcasted_iota(jnp.int32, (TPR, N_ROW, NB), 2).astype(jnp.float32)
    places = (cell_ids + jax.random.uniform(jitter_key, (TPR, N_ROW, NB), jnp.float32, 0.0, 0.9)) / NB
    amplitude = jax.random.uniform(scale_key, (TPR, N_ROW, NB), jnp.float32, scale_lo, scale_hi)
    distance = jnp.abs(places[:, :, :, None] - places[:, :, None, :])
    kernel = amplitude[:, :, :, None] * amplitude[:, :, None, :] * jnp.exp(-distance / length)
    spread = 0.01
    noise = jax.random.uniform(noise_key, (TPR, N_ROW, NB, NB), jnp.float32, -spread, spread)
    noise = 0.5 * (noise + jnp.swapaxes(noise, 2, 3))
    nugget = jax.random.uniform(nugget_key, (TPR, N_ROW, NB, 1), jnp.float32, 1.0, 3.0)
    row_ids = lax.broadcasted_iota(jnp.int32, (TPR, N_ROW, NB, NB), 2)
    col_ids = lax.broadcasted_iota(jnp.int32, (TPR, N_ROW, NB, NB), 3)
    return kernel + noise + jnp.where(row_ids == col_ids, nugget, 0.0)


def draw_diag_tiles(key, part):
    left_factor, right_factor, ranks = panel_draw(key)
    key = jax.random.fold_in(key, 4)
    column_ids = lax.broadcasted_iota(jnp.int32, (TPR, N_ROW, NB, R), 3)
    keep_mask = column_ids < ranks[:, :, None, None]
    left_kept = jnp.where(keep_mask, left_factor.astype(jnp.bfloat16).astype(jnp.float32), 0.0)
    right_kept = jnp.where(keep_mask, right_factor.astype(jnp.bfloat16).astype(jnp.float32), 0.0)
    highest = lax.Precision.HIGHEST
    cores = jnp.einsum('panr,pans->pars', right_kept, right_kept, precision=highest)
    inner = jnp.einsum('panr,pars->pans', left_kept, cores, precision=highest)
    correction = jnp.einsum('pans,pams->panm', inner, left_kept, precision=highest)
    base = matern_base(key, 0.1, 0.7, 1.4)
    return (base + correction).astype(jnp.float32)


def draw_column_rank(key, part):
    key = jax.random.fold_in(key, 6)
    return rank_draw(key)


def level_of(key, shape, cuts, least, top_value):
    def one(position, blocks):
        steps = jax.random.uniform(jax.random.fold_in(jax.random.fold_in(key, 6), position), (blocks,), jnp.float32, least / len(cuts), top_value / len(cuts))
        return jnp.repeat(jnp.exp(steps), shape[position] // blocks).reshape((-1,) + (1,) * (len(shape) - position - 1))

    level = one(*cuts[0])
    for cut in cuts[1:]:
        level = level * one(*cut)
    return level


def centred(rng, dims, scale, limit, pieces=(), dtype=jnp.bfloat16):
    factor_of = level_of(rng, dims, pieces, -0.22, 0.18) if pieces else 1.0
    result = jax.random.normal(rng, dims, jnp.float32) * scale * factor_of
    return jnp.minimum(jnp.maximum(result, -limit), limit).astype(dtype)


def setup_inputs(seed: int = 0) -> dict:
    arg_keys = jax.random.split(jax.random.key(seed), 7)
    pan_left = draw_pan_left(jax.random.fold_in(arg_keys[6], 71), 0)
    pan_right = draw_pan_right(jax.random.fold_in(arg_keys[6], 71), 0)
    panel_rank = draw_panel_rank(jax.random.fold_in(arg_keys[6], 71), 0)
    diag_tiles = draw_diag_tiles(jax.random.fold_in(arg_keys[6], 71), 0)
    col_right = centred(arg_keys[4], (TPR, N_ROW, R, NB), 1.0, 6.0, ((1, 16), (2, 16)))
    column_rank = draw_column_rank(jax.random.fold_in(arg_keys[6], 71), 0)
    return {"pan_left": pan_left, "pan_right": pan_right, "panel_rank": panel_rank, "diag_tiles": diag_tiles, "col_right": col_right, "column_rank": column_rank}


def reference(pan_left, pan_right, panel_rank, diag_tiles, col_right, column_rank):
    tile_count = TPR * N_ROW
    left_factor = pan_left.reshape(tile_count, NB, R)
    right_factor = pan_right.reshape(tile_count, NB, R)
    rank_limit = panel_rank.reshape(tile_count, 1, 1)
    column_ids = lax.broadcasted_iota(jnp.int32, (tile_count, NB, R), 2)
    left_factor = jnp.where(column_ids < rank_limit, left_factor, jnp.zeros_like(left_factor))
    right_factor = jnp.where(column_ids < rank_limit, right_factor, jnp.zeros_like(right_factor))
    stacked = right_factor.transpose(0, 2, 1).reshape(tile_count * R, NB)
    gram_cores = jnp.dot(stacked.astype(jnp.float32), stacked.T.astype(jnp.float32), preferred_element_type=jnp.float32).astype(jnp.bfloat16)
    gram_cores = gram_cores.reshape(tile_count, R, tile_count, R).astype(jnp.float32)
    left_wide = left_factor.astype(jnp.float32)
    tile_update = jnp.einsum('inr,irjs->ijns', left_wide, gram_cores)
    tile_ids = jnp.arange(tile_count)
    lower_mask = (tile_ids[:, None] > tile_ids[None, :])[:, :, None, None]
    panel_update = jnp.where(lower_mask, tile_update, jnp.zeros_like(tile_update)).astype(jnp.bfloat16)
    panel_update = panel_update.reshape(TPR, N_ROW, TPC, N_COL, NB, R)
    own_cores = jnp.einsum('iris->irs', gram_cores)
    products = jnp.einsum('inr,irs->ins', left_wide, own_cores).astype(jnp.bfloat16)
    correction = jnp.einsum('ins,ims->inm', products.astype(jnp.float32), left_wide)
    diag_new = diag_tiles.reshape(tile_count, NB, NB) - correction
    lead_factor = jnp.linalg.cholesky(diag_new[0])
    right_ids = lax.broadcasted_iota(jnp.int32, (tile_count, R, NB), 1)
    row_ids = lax.broadcasted_iota(jnp.int32, (tile_count, R, NB), 0)
    keep_mask = (right_ids < column_rank.reshape(tile_count, 1, 1)) & (row_ids >= 1)
    flat_right = col_right.reshape(tile_count, R, NB)
    right_kept = jnp.where(keep_mask, flat_right, jnp.zeros_like(flat_right))
    right_side = right_kept.astype(jnp.float32).reshape(tile_count * R, NB).T
    solution = lax.linalg.triangular_solve(lead_factor, right_side, left_side=True, lower=True)
    col_solved = solution.T.reshape(TPR, N_ROW, R, NB)
    return (panel_update, diag_new.reshape(TPR, N_ROW, NB, NB), lead_factor, col_solved)
```

```python
import jax, jax.numpy as jnp
from jax import lax
from jax.sharding import PartitionSpec as P
from jax.experimental import pallas as pl
from jax.experimental.pallas import tpu as pltpu

BLK = 128
GRP = 8

def recip(value):
    start = pl.reciprocal(value, approx=True)
    return start * (2.0 - value * start)

def invert_factor(rows):
    count = len(rows)
    lanes = lax.broadcasted_iota(jnp.int32, (GRP, BLK), 1)
    subs = lax.broadcasted_iota(jnp.int32, (GRP, BLK), 0)
    shape = (GRP, BLK)
    rows = list(rows)
    out = []
    for g in range(count):
        base = g * GRP
        here = (lanes >= base) & (lanes < base + GRP)
        cols = {
            h: [jnp.broadcast_to(rows[h][:, base + j : base + j + 1], shape) for j in range(GRP)]
            for h in range(g, count)
        }
        tri = {
            (i, j): jnp.broadcast_to(cols[g][j][i : i + 1, :], shape)
            for j in range(GRP)
            for i in range(j, GRP)
        }
        pivot = jnp.where(here, jnp.where(lanes - base == subs, 1.0, 0.0), rows[g])
        lines = [jnp.broadcast_to(pivot[j : j + 1, :], shape) for j in range(GRP)]
        inv = []
        unit = {}
        for j in range(GRP):
            inv.append(recip(tri[j, j]))
            for i in range(j + 1, GRP):
                unit[i, j] = tri[i, j] * inv[j]
            for i in range(j + 1, GRP):
                for k in range(j + 1, i + 1):
                    tri[i, k] = tri[i, k] - unit[i, j] * tri[k, j]
                lines[i] = lines[i] - unit[i, j] * lines[j]
        done = lines[0] * lax.rsqrt(tri[0, 0])
        for j in range(1, GRP):
            done = jnp.where(subs == j, lines[j] * lax.rsqrt(tri[j, j]), done)
        out.append(jnp.where(lanes <= subs + base, done, 0.0))
        if g + 1 < count:
            back = [None] * GRP
            for j in range(GRP - 1, -1, -1):
                acc = lines[j] * inv[j]
                for i in range(GRP - 1, j, -1):
                    acc = acc - unit[i, j] * back[i]
                back[j] = acc
            for h in range(g + 1, count):
                acc = jnp.where(here, 0.0, rows[h])
                for j in range(GRP - 1, -1, -1):
                    acc = acc - cols[h][j] * back[j]
                rows[h] = acc
    return out

NT = (((1,), (1,)), ((), ()))

def halves(value):
    high = value.astype(jnp.bfloat16)
    return high, (value - high.astype(jnp.float32)).astype(jnp.bfloat16)

def mul3(lh, ll, rh, rl):
    def one(x, y):
        return lax.dot_general(x, y, NT, preferred_element_type=jnp.float32)
    return one(lh, rh) + (one(lh, rl) + one(ll, rh))

def chol_kernel(pos_ref, lead_ref, y_ref, x_ref, part_ref, high, low, work, wh, wl):
    order = y_ref.shape[1]
    count = order // BLK
    extra = y_ref.shape[0]
    total = order + extra
    row, col = pos_ref[0], pos_ref[1]

    def block_of(i, k):
        apart = i - k
        source, slot = (i, apart) if 2 * apart <= count else (k, count - apart)
        return lead_ref[source % 2, source // 2, slot]

    def given(r0, r1, k):
        lo = k * BLK
        parts = [block_of(r // BLK, k) for r in range(r0, min(r1, order), BLK)]
        if r1 > order:
            parts.append(y_ref[max(r0, order) - order:r1 - order, lo:lo + BLK])
        return parts[0] if len(parts) == 1 else jnp.concatenate(parts, axis=0)

    for r in range(0, order, BLK):
        work[r:r + BLK, :] = block_of(r // BLK, 0)
    work[order:, :] = y_ref[:, :BLK]
    part_ref[...] = jnp.zeros_like(part_ref)

    def spans(start):
        return [(r, min(r + 2 * BLK, total)) for r in range(start, total, 2 * BLK)]

    def step(k, carry):
        base = pl.multiple_of(k * BLK, BLK)
        rows = [work[pl.ds(base + g * GRP, GRP), :] for g in range(BLK // GRP)]
        inverse = invert_factor(rows)
        full = jnp.concatenate(inverse, axis=0)
        high_part, low_part = halves(full)
        wh[...] = high_part
        wl[...] = low_part

        for s in range(count):
            @pl.when(k == s)
            def _(s=s):
                lo, hi = s * BLK, s * BLK + BLK
                for r0, r1 in spans(lo):
                    sh, sl = halves(work[r0:r1, :])
                    panel = mul3(sh, sl, wh[...], wl[...])
                    ph, pl_ = halves(panel)
                    high[r0:r1, lo:hi] = ph
                    low[r0:r1, lo:hi] = pl_
                    work[r0:r1, :] = panel
                x_ref[:, lo:hi] = work[order:order + x_ref.shape[0], :]

                @pl.when(jnp.logical_and(col == s, row >= s))
                def _():
                    block = work[pl.ds(pl.multiple_of(row * BLK, BLK), BLK), :]
                    r = lax.broadcasted_iota(jnp.int32, (BLK, BLK), 0)
                    c = lax.broadcasted_iota(jnp.int32, (BLK, BLK), 1)
                    part_ref[...] = jnp.where((row > s) | (r >= c), block, 0.0)

                if s + 1 < count:
                    for r0, r1 in spans(hi):
                        work[r0:r1, :] = given(r0, r1, s + 1) - mul3(
                            high[r0:r1, :hi], low[r0:r1, :hi],
                            high[hi:hi + BLK, :hi], low[hi:hi + BLK, :hi])
        return carry

    lax.fori_loop(0, count, step, 0)

def chol_call(pos, lead, right, count):
    extra, order = right.shape
    vm = pl.BlockSpec(memory_space=pltpu.VMEM)
    return pl.pallas_call(
        chol_kernel,
        out_shape=(jax.ShapeDtypeStruct((count, order), jnp.float32), jax.ShapeDtypeStruct((BLK, BLK), jnp.float32)),
        in_specs=[pl.BlockSpec(memory_space=pltpu.SMEM), vm, vm],
        out_specs=(vm, vm),
        scratch_shapes=[
            pltpu.VMEM((order + extra, order), jnp.bfloat16),
            pltpu.VMEM((order + extra, order), jnp.bfloat16),
            pltpu.VMEM((order + extra, BLK), jnp.float32),
            pltpu.VMEM((BLK, BLK), jnp.bfloat16),
            pltpu.VMEM((BLK, BLK), jnp.bfloat16),
        ],
        compiler_params=pltpu.CompilerParams(vmem_limit_bytes=58 * 2**20),
        cost_estimate=pl.CostEstimate(flops=10**11, bytes_accessed=2 * 10**8, transcendentals=0),
    )(pos, lead, right)


def exchange_kernel(
    vu_ref, diag_ref, vu_all, vv_all, lead,
    blocks, piece, pairs, um,
    uv_send, uv_recv, fw_send, fw_recv, cut_send, cut_recv, ring_send, ring_recv,
    flat_send, flat_recv, pair_send, pair_recv, vcut_send, vcut_recv, vflat_send, vflat_recv, local_sem,
):
    rows, cols = flat_send.shape[0], vu_all.shape[0]
    depth = cols // 2
    thin = piece.shape[2]
    band = lead.shape[2]
    p, c = lax.axis_index("row"), lax.axis_index("col")
    z, core = c // 2, lax.rem(c, 2)
    sibling = c + 1 - 2 * core

    def along(d):
        return (p, 2 * lax.rem(z + d, depth) + core)

    def plane(d):
        return (lax.rem(p + d, rows), c)

    def remote(src, dst, send, recv, where):
        return pltpu.make_async_remote_copy(
            src_ref=src, dst_ref=dst, send_sem=send, recv_sem=recv,
            device_id=where, device_id_type=pl.DeviceIdType.MESH,
        )

    barrier = pltpu.get_barrier_semaphore()
    partners = [along(d) for d in range(1, depth)] + [(p, sibling)] + [plane(d) for d in range(1, rows)]
    for where in partners:
        pl.semaphore_signal(barrier, inc=1, device_id=where, device_id_type=pl.DeviceIdType.MESH)
    pl.semaphore_wait(barrier, len(partners))

    pending = []

    def spread_start(a):
        first = []
        for d in range(1, depth):
            copy = remote(vu_ref.at[a], vu_all.at[c, a], uv_send.at[a, d], uv_recv.at[a, d], along(d))
            copy.start()
            first.append(copy)
        own = remote(vu_ref.at[a], vu_all.at[c, a], fw_send.at[a, 0], fw_recv.at[a, 0], (p, sibling))
        own.start()
        vu_all[c, a] = vu_ref[a]
        return first, own

    def spread_end(a, first, own):
        later = [own]
        for d in range(1, depth):
            first[d - 1].wait_recv()
            held = vu_all.at[2 * lax.rem(z + depth - d, depth) + core, a]
            copy = remote(held, held, fw_send.at[a, d], fw_recv.at[a, d], (p, sibling))
            copy.start()
            later.append(copy)
        for copy in later:
            copy.wait_recv()
        pending.extend(first + later)

    first, own = spread_start(0)
    spread_end(0, first, own)

    cuts = [
        remote(blocks.at[:, pl.ds(d * thin, thin), :], piece.at[z], cut_send.at[d], cut_recv, (d, c))
        for d in range(1, rows)
    ]

    @pl.when(p == 0)
    def _():
        size = BLK
        r = lax.broadcasted_iota(jnp.int32, (size, size), 0)
        l = lax.broadcasted_iota(jnp.int32, (size, size), 1)
        half = size // 2

        def dots(x, y, dims):
            return lax.dot_general(x, y, (dims, ((), ())), preferred_element_type=jnp.float32)

        gram = jnp.zeros((size, size), jnp.float32)
        for s in range(cols):
            slab = vu_all[s, 0]
            gram = gram + dots(slab, slab, ((0,), (0,)))
        core_w = jnp.where((r < half) & (l < half), gram, 0.0).astype(jnp.bfloat16)
        down = jnp.where(r == l + half, 1.0, 0.0).astype(jnp.bfloat16)
        right = jnp.where(l == r + half, 1.0, 0.0).astype(jnp.bfloat16)
        same = jnp.where((r == l) & (r >= half), 1.0, 0.0)
        low_w = dots(down, core_w, ((1,), (0,)))
        low_w16 = low_w.astype(jnp.bfloat16)
        take_mu = (low_w + same).astype(jnp.bfloat16)
        take_um = (dots(low_w16, right, ((1,), (0,))) + down.astype(jnp.float32)).astype(jnp.bfloat16)
        for s in range(cols):
            um[s] = dots(vu_all[s, 0], take_um, ((1,), (0,))).astype(jnp.bfloat16)
        mine = dots(vu_ref[0], take_mu, ((1,), (0,))).astype(jnp.bfloat16)
        for j in range(band):
            other = lax.rem(c + cols - j, cols)
            fix = dots(mine, um[other], ((1,), (1,)))
            block = diag_ref[:, pl.ds(pl.multiple_of(other * size, size), size)] - 0.5 * fix

            @pl.when(c >= j)
            def _(block=block, j=j):
                blocks[j] = block

            @pl.when(c < j)
            def _(block=block, j=j):
                blocks[j] = block.T
        piece[z] = blocks[:, :thin, :]
        for copy in cuts:
            copy.start()

    @pl.when(p > 0)
    def _():
        cuts[0].wait_recv()

    ring = []
    for d in range(1, depth):
        copy = remote(piece.at[z], piece.at[z], ring_send.at[d], ring_recv.at[d], along(d))
        copy.start()
        ring.append(copy)
    first, own = spread_start(1)
    for copy in ring:
        copy.wait_recv()

    def place(q):
        return lead.at[core, :, :, pl.ds(pl.multiple_of(q * thin, thin), thin), :]

    flats = []
    for d in range(1, rows):
        copy = remote(piece, place(p), flat_send.at[d], flat_recv.at[d], plane(d))
        copy.start()
        flats.append(copy)
    keep = pltpu.make_async_copy(piece, place(p), local_sem)
    keep.start()
    halfway = [remote(piece, place(p), pair_send.at[0], pair_recv.at[0], (p, sibling))]
    halfway[0].start()

    spread_end(1, first, own)
    vcuts = [remote(pairs.at[d], vv_all.at[lax.rem(p + d, rows)], vcut_send.at[d], vcut_recv, plane(d)) for d in range(1, rows)]

    @pl.when(p == c)
    def _():
        for s in range(cols):
            d = lax.rem(s + rows - p, rows)
            lanes = lax.broadcasted_iota(jnp.int32, (BLK, BLK), 1)
            lefts = vu_all[s, 0].astype(jnp.float32)
            rights = pltpu.roll(vu_all[s, 1].astype(jnp.float32), BLK // 2, 1)
            pairs[d] = jnp.where(lanes < BLK // 2, lefts, rights).astype(jnp.bfloat16)
        vv_all[p] = pairs[0]
        for copy in vcuts:
            copy.start()

    @pl.when(p != c)
    def _():
        vcuts[0].wait_recv()

    vflats = []
    for d in range(1, rows):
        copy = remote(vv_all.at[p], vv_all.at[p], vflat_send.at[d], vflat_recv.at[d], plane(d))
        copy.start()
        vflats.append(copy)

    for d in range(1, rows):
        flats[d - 1].wait_recv()
        held = place(lax.rem(p + rows - d, rows))
        copy = remote(held, held, pair_send.at[d], pair_recv.at[d], (p, sibling))
        copy.start()
        halfway.append(copy)
    keep.wait()
    for copy in halfway + vflats:
        copy.wait_recv()
    for copy in pending + ring + flats + halfway + vflats:
        copy.wait_send()

    @pl.when(p == 0)
    def _():
        for copy in cuts:
            copy.wait_send()

    @pl.when(p == c)
    def _():
        for copy in vcuts:
            copy.wait_send()


def exchange(vu, diag_rows):
    rows, cols = lax.axis_size("row"), lax.axis_size("col")
    depth, band, thin = cols // 2, cols // 2 + 1, BLK // rows
    vm = pl.BlockSpec(memory_space=pltpu.VMEM)
    dma = pltpu.SemaphoreType.DMA
    return pl.pallas_call(
        exchange_kernel,
        out_shape=(
            jax.ShapeDtypeStruct((cols, 2, BLK, BLK), jnp.bfloat16),
            jax.ShapeDtypeStruct((cols, BLK, BLK), jnp.bfloat16),
            jax.ShapeDtypeStruct((2, depth, band, BLK, BLK), jnp.float32),
        ),
        in_specs=[vm, vm],
        out_specs=(vm, vm, pl.BlockSpec(memory_space=pl.ANY)),
        scratch_shapes=[
            pltpu.VMEM((band, BLK, BLK), jnp.float32),
            pltpu.VMEM((depth, band, thin, BLK), jnp.float32),
            pltpu.VMEM((cols, BLK, BLK), jnp.bfloat16),
            pltpu.VMEM((cols, BLK, BLK), jnp.bfloat16),
            dma((2, depth)), dma((2, depth)), dma((2, depth)), dma((2, depth)),
            dma((rows,)), dma, dma((depth,)), dma((depth,)),
            dma((rows,)), dma((rows,)), dma((rows,)), dma((rows,)),
            dma((rows,)), dma, dma((rows,)), dma((rows,)), dma,
        ],
        compiler_params=pltpu.CompilerParams(
            collective_id=0, has_side_effects=True, vmem_limit_bytes=40 * 2**20
        ),
    )(vu, diag_rows)


def body(pan_left, pan_right, panel_rank, diag_tiles, col_right, column_rank):
    tile_rows = pan_left.shape[0]
    slab_rows = pan_left.shape[2]
    rank_width = pan_left.shape[3]
    tile_order = diag_tiles.shape[3]
    row_count = lax.axis_size("row")
    col_count = lax.axis_size("col")
    row_index = lax.axis_index("row")
    col_index = lax.axis_index("col")
    col_tiles = tile_rows * row_count // col_count
    columns = lax.broadcasted_iota(jnp.int32, pan_left.shape, 3)
    keep_mask = columns < panel_rank[:, :, None, None]
    zeros_half = jnp.zeros_like(pan_left)
    left_masked = jnp.where(keep_mask, pan_left, zeros_half)
    right_masked = jnp.where(keep_mask, pan_right, zeros_half)
    vu = jnp.concatenate([right_masked, left_masked], axis=3)[:, 0]
    vu_all, vv_all, lead = exchange(vu, diag_tiles[0, 0])
    flat_vu = vu_all.transpose(1, 0, 2, 3).reshape(tile_rows, tile_order, 2 * rank_width)
    right_tiles, left_tiles = flat_vu[:, :, :rank_width], flat_vu[:, :, rank_width:]
    theirs = vv_all.reshape(tile_order, col_tiles, rank_width)
    own_gram = jnp.einsum(
        "anr,ans->ars", right_tiles, right_tiles, preferred_element_type=jnp.float32
    ).astype(jnp.bfloat16)
    products = jnp.einsum(
        "anr,ars->ans", left_tiles, own_gram, preferred_element_type=jnp.float32
    ).astype(jnp.bfloat16)
    product_rows = lax.dynamic_slice_in_dim(products, col_index * slab_rows, slab_rows, 1)
    correction = jnp.einsum(
        "ans,ams->anm", product_rows, left_tiles, preferred_element_type=jnp.float32
    )
    diag_new = diag_tiles - correction[:, None]
    cross_gram = jnp.einsum(
        "anr,nbs->abrs", right_tiles, theirs, preferred_element_type=jnp.float32
    ).astype(jnp.bfloat16)

    narrow_rows = col_right.shape[2]
    rank_ids = lax.broadcasted_iota(jnp.int32, col_right.shape, 2) + col_index * narrow_rows
    tile_ids = lax.broadcasted_iota(jnp.int32, col_right.shape, 0) * row_count + row_index
    keep_right = (rank_ids < column_rank[:, :, None, None]) & (tile_ids >= 1)
    right_kept = jnp.where(keep_right, col_right, jnp.zeros_like(col_right))
    right_side = right_kept.astype(jnp.float32).reshape(-1, tile_order)
    count = right_side.shape[0]
    right_side = jnp.pad(right_side, ((0, -count % 16), (0, 0)))
    place = jnp.stack([row_index, col_index]).astype(jnp.int32)
    solved, lead_part = chol_call(place, lead, right_side, count)
    col_solved = solved.reshape(col_right.shape)

    tile_update = jnp.einsum(
        "anr,abrs->abns", left_tiles, cross_gram, preferred_element_type=jnp.float32
    )
    row_ids = lax.broadcasted_iota(jnp.int32, (tile_rows, col_tiles), 0) * row_count + row_index
    col_ids = lax.broadcasted_iota(jnp.int32, (tile_rows, col_tiles), 1) * col_count + col_index
    lower_mask = (row_ids > col_ids)[:, :, None, None]
    panel_update = jnp.where(lower_mask, tile_update, jnp.zeros_like(tile_update)).astype(
        jnp.bfloat16
    )
    panel_update = panel_update.reshape(tile_rows, 1, col_tiles, 1, tile_order, rank_width)
    return (panel_update, diag_new, lead_part, col_solved)


def solution(mesh):
    placed = (
        P(None, "row", "col", None),
        P(None, "row", "col", None),
        P(None, "row"),
        P(None, "row", "col", None),
        P(None, "row", "col", None),
        P(None, "row"),
    )
    return jax.shard_map(
        body,
        mesh=mesh,
        in_specs=placed,
        out_specs=(
            P(None, "row", None, "col", None, None),
            P(None, "row", "col", None),
            P("row", "col"),
            P(None, "row", "col", None),
        ),
        check_vma=False,
    )
```

```python
import jax, jax.numpy as jnp
from jax import lax
from jax.sharding import PartitionSpec as P
from jax.experimental import pallas as pl
from jax.experimental.pallas import tpu as pltpu

BLK = 128
GRP = 8

def recip(value):
    start = pl.reciprocal(value, approx=True)
    return start * (2.0 - value * start)

def invert_factor(rows):
    count = len(rows)
    lanes = lax.broadcasted_iota(jnp.int32, (GRP, BLK), 1)
    subs = lax.broadcasted_iota(jnp.int32, (GRP, BLK), 0)
    shape = (GRP, BLK)
    rows = list(rows)
    out = []
    for g in range(count):
        base = g * GRP
        here = (lanes >= base) & (lanes < base + GRP)
        cols = {
            h: [jnp.broadcast_to(rows[h][:, base + j : base + j + 1], shape) for j in range(GRP)]
            for h in range(g, count)
        }
        tri = {
            (i, j): jnp.broadcast_to(cols[g][j][i : i + 1, :], shape)
            for j in range(GRP)
            for i in range(j, GRP)
        }
        pivot = jnp.where(here, jnp.where(lanes - base == subs, 1.0, 0.0), rows[g])
        lines = [jnp.broadcast_to(pivot[j : j + 1, :], shape) for j in range(GRP)]
        inv = []
        unit = {}
        for j in range(GRP):
            inv.append(recip(tri[j, j]))
            for i in range(j + 1, GRP):
                unit[i, j] = tri[i, j] * inv[j]
            for i in range(j + 1, GRP):
                for k in range(j + 1, i + 1):
                    tri[i, k] = tri[i, k] - unit[i, j] * tri[k, j]
                lines[i] = lines[i] - unit[i, j] * lines[j]
        done = lines[0] * lax.rsqrt(tri[0, 0])
        for j in range(1, GRP):
            done = jnp.where(subs == j, lines[j] * lax.rsqrt(tri[j, j]), done)
        out.append(jnp.where(lanes <= subs + base, done, 0.0))
        if g + 1 < count:
            back = [None] * GRP
            for j in range(GRP - 1, -1, -1):
                acc = lines[j] * inv[j]
                for i in range(GRP - 1, j, -1):
                    acc = acc - unit[i, j] * back[i]
                back[j] = acc
            for h in range(g + 1, count):
                acc = jnp.where(here, 0.0, rows[h])
                for j in range(GRP - 1, -1, -1):
                    acc = acc - cols[h][j] * back[j]
                rows[h] = acc
    return out

NT = (((1,), (1,)), ((), ()))

def halves(value):
    high = value.astype(jnp.bfloat16)
    return high, (value - high.astype(jnp.float32)).astype(jnp.bfloat16)

def mul3(lh, ll, rh, rl):
    def one(x, y):
        return lax.dot_general(x, y, NT, preferred_element_type=jnp.float32)
    return one(lh, rh) + (one(lh, rl) + one(ll, rh))

def chol_kernel(pos_ref, lead_ref, y_ref, x_ref, part_ref, high, low, work, wh, wl):
    order = y_ref.shape[1]
    count = order // BLK
    extra = y_ref.shape[0]
    total = order + extra
    row, col = pos_ref[0], pos_ref[1]

    def block_of(i, k):
        apart = i - k
        source, slot = (i, apart) if 2 * apart <= count else (k, count - apart)
        return lead_ref[source % 2, (source // 2) * (count // 2 + 1) + slot]

    def given(r0, r1, k):
        lo = k * BLK
        parts = [block_of(r // BLK, k) for r in range(r0, min(r1, order), BLK)]
        if r1 > order:
            parts.append(y_ref[max(r0, order) - order:r1 - order, lo:lo + BLK])
        return parts[0] if len(parts) == 1 else jnp.concatenate(parts, axis=0)

    for r in range(0, order, BLK):
        work[r:r + BLK, :] = block_of(r // BLK, 0)
    work[order:, :] = y_ref[:, :BLK]
    part_ref[...] = jnp.zeros_like(part_ref)

    def spans(start):
        return [(r, min(r + 2 * BLK, total)) for r in range(start, total, 2 * BLK)]

    def step(k, carry):
        base = pl.multiple_of(k * BLK, BLK)
        rows = [work[pl.ds(base + g * GRP, GRP), :] for g in range(BLK // GRP)]
        inverse = invert_factor(rows)
        full = jnp.concatenate(inverse, axis=0)
        high_part, low_part = halves(full)
        wh[...] = high_part
        wl[...] = low_part

        for s in range(count):
            @pl.when(k == s)
            def _(s=s):
                lo, hi = s * BLK, s * BLK + BLK
                for r0, r1 in spans(lo):
                    sh, sl = halves(work[r0:r1, :])
                    panel = mul3(sh, sl, wh[...], wl[...])
                    ph, pl_ = halves(panel)
                    high[r0:r1, lo:hi] = ph
                    low[r0:r1, lo:hi] = pl_
                    work[r0:r1, :] = panel
                x_ref[:, lo:hi] = work[order:order + x_ref.shape[0], :]

                @pl.when(jnp.logical_and(col == s, row >= s))
                def _():
                    block = work[pl.ds(pl.multiple_of(row * BLK, BLK), BLK), :]
                    r = lax.broadcasted_iota(jnp.int32, (BLK, BLK), 0)
                    c = lax.broadcasted_iota(jnp.int32, (BLK, BLK), 1)
                    part_ref[...] = jnp.where((row > s) | (r >= c), block, 0.0)

                if s + 1 < count:
                    for r0, r1 in spans(hi):
                        work[r0:r1, :] = given(r0, r1, s + 1) - mul3(
                            high[r0:r1, :hi], low[r0:r1, :hi],
                            high[hi:hi + BLK, :hi], low[hi:hi + BLK, :hi])
        return carry

    lax.fori_loop(0, count, step, 0)

def chol_call(pos, lead, right, count):
    extra, order = right.shape
    vm = pl.BlockSpec(memory_space=pltpu.VMEM)
    return pl.pallas_call(
        chol_kernel,
        out_shape=(jax.ShapeDtypeStruct((count, order), jnp.float32), jax.ShapeDtypeStruct((BLK, BLK), jnp.float32)),
        in_specs=[pl.BlockSpec(memory_space=pltpu.SMEM), vm, vm],
        out_specs=(vm, vm),
        scratch_shapes=[
            pltpu.VMEM((order + extra, order), jnp.bfloat16),
            pltpu.VMEM((order + extra, order), jnp.bfloat16),
            pltpu.VMEM((order + extra, BLK), jnp.float32),
            pltpu.VMEM((BLK, BLK), jnp.bfloat16),
            pltpu.VMEM((BLK, BLK), jnp.bfloat16),
        ],
        compiler_params=pltpu.CompilerParams(vmem_limit_bytes=58 * 2**20),
        cost_estimate=pl.CostEstimate(flops=10**11, bytes_accessed=2 * 10**8, transcendentals=0),
    )(pos, lead, right)


def exchange_kernel(
    vu_ref, diag_ref, vu_all, vv_all, lead,
    blocks, piece, pairs, um,
    uv_send, uv_recv, fw_send, fw_recv, cut_send, cut_recv, ring_send, ring_recv,
    flat_send, flat_recv, pair_send, pair_recv, vcut_send, vcut_recv, vflat_send, vflat_recv, local_sem,
):
    rows, cols = cut_send.shape[0], vu_all.shape[0]
    side = {4: 2, 16: 4}[rows]
    depth = cols // 2
    band = cols // 2 + 1
    slots = depth * band
    thin = piece.shape[1]
    p, c = lax.axis_index("row"), lax.axis_index("col")
    z, core = c // 2, lax.rem(c, 2)
    sibling = c + 1 - 2 * core

    def along(d):
        return (p, 2 * lax.rem(z + d, depth) + core)

    def shift(q, axis, steps):
        x, y = q // side, lax.rem(q, side)
        if axis == 0:
            return lax.rem(x + steps + side, side) * side + y
        return x * side + lax.rem(y + steps + side, side)

    def remote(src, dst, send, recv, where):
        return pltpu.make_async_remote_copy(
            src_ref=src, dst_ref=dst, send_sem=send, recv_sem=recv,
            device_id=where, device_id_type=pl.DeviceIdType.MESH,
        )

    barrier = pltpu.get_barrier_semaphore()
    partners = [along(d) for d in range(1, depth)] + [(p, sibling)] + [(lax.rem(p + d, rows), c) for d in range(1, rows)]
    for where in partners:
        pl.semaphore_signal(barrier, inc=1, device_id=where, device_id_type=pl.DeviceIdType.MESH)
    pl.semaphore_wait(barrier, len(partners))

    pending = []

    def spread_start(a):
        first = []
        for d in range(1, depth):
            copy = remote(vu_ref.at[a], vu_all.at[c, a], uv_send.at[a, d], uv_recv.at[a, d], along(d))
            copy.start()
            first.append(copy)
        own = remote(vu_ref.at[a], vu_all.at[c, a], fw_send.at[a, 0], fw_recv.at[a, 0], (p, sibling))
        own.start()
        vu_all[c, a] = vu_ref[a]
        return first, own

    def spread_end(a, first, own):
        later = [own]
        for d in range(1, depth):
            first[d - 1].wait_recv()
            held = vu_all.at[2 * lax.rem(z + depth - d, depth) + core, a]
            copy = remote(held, held, fw_send.at[a, d], fw_recv.at[a, d], (p, sibling))
            copy.start()
            later.append(copy)
        for copy in later:
            copy.wait_recv()
        pending.extend(first + later)

    first, own = spread_start(0)
    spread_end(0, first, own)

    mine_slots = pl.ds(z * band, band)
    cuts = [
        remote(blocks.at[:, pl.ds(d * thin, thin), :], piece.at[mine_slots], cut_send.at[d], cut_recv, (d, c))
        for d in range(1, rows)
    ]

    @pl.when(p == 0)
    def _():
        size = BLK
        r = lax.broadcasted_iota(jnp.int32, (size, size), 0)
        l = lax.broadcasted_iota(jnp.int32, (size, size), 1)
        half = size // 2

        def dots(x, y, dims):
            return lax.dot_general(x, y, (dims, ((), ())), preferred_element_type=jnp.float32)

        gram = jnp.zeros((size, size), jnp.float32)
        for s in range(cols):
            slab = vu_all[s, 0]
            gram = gram + dots(slab, slab, ((0,), (0,)))
        core_w = jnp.where((r < half) & (l < half), gram, 0.0).astype(jnp.bfloat16)
        down = jnp.where(r == l + half, 1.0, 0.0).astype(jnp.bfloat16)
        right = jnp.where(l == r + half, 1.0, 0.0).astype(jnp.bfloat16)
        same = jnp.where((r == l) & (r >= half), 1.0, 0.0)
        low_w = dots(down, core_w, ((1,), (0,)))
        low_w16 = low_w.astype(jnp.bfloat16)
        take_mu = (low_w + same).astype(jnp.bfloat16)
        take_um = (dots(low_w16, right, ((1,), (0,))) + down.astype(jnp.float32)).astype(jnp.bfloat16)
        for s in range(cols):
            um[s] = dots(vu_all[s, 0], take_um, ((1,), (0,))).astype(jnp.bfloat16)
        mine = dots(vu_ref[0], take_mu, ((1,), (0,))).astype(jnp.bfloat16)
        for j in range(band):
            other = lax.rem(c + cols - j, cols)
            fix = dots(mine, um[other], ((1,), (1,)))
            block = diag_ref[:, pl.ds(pl.multiple_of(other * size, size), size)] - 0.5 * fix

            @pl.when(c >= j)
            def _(block=block, j=j):
                blocks[j] = block

            @pl.when(c < j)
            def _(block=block, j=j):
                blocks[j] = block.T
        piece[mine_slots] = blocks[:, :thin, :]
        for copy in cuts:
            copy.start()

    @pl.when(p > 0)
    def _():
        cuts[0].wait_recv()

    ring = []
    for d in range(1, depth):
        copy = remote(piece.at[mine_slots], piece.at[mine_slots], ring_send.at[d], ring_recv.at[d], along(d))
        copy.start()
        ring.append(copy)
    for copy in ring:
        copy.wait_recv()
    first, own = spread_start(1)

    middle, quarter = slots // 2, slots // 4
    edges = [(0, quarter, middle), (middle, middle + quarter, slots)]

    def lead_region(q, k, part):
        lo, mid, hi = edges[k]
        lo, hi = {None: (lo, hi), 0: (lo, mid), 1: (mid, hi)}[part]
        return lead.at[core, pl.ds(lo, hi - lo), pl.ds(pl.multiple_of(q * thin, thin), thin), :]

    def piece_region(q, k, part):
        lo, mid, hi = edges[k]
        return piece.at[pl.ds(lo, hi - lo)]

    def pair_region(q, k, part):
        half = BLK // 2
        lo, size = {None: (0, half), 0: (0, half // 2), 1: (half // 2, half // 2)}[part]
        return vv_all.at[q, pl.ds(k * half + lo, size)]

    def plane_gather(region, origin, send, recv, shared):
        copies, siblings = [], []
        ring_of = [(1 - k, k) for k in range(2)]

        def go(k, slot, src, dst, axis, steps):
            copy = remote(src, dst, send.at[k, slot], recv.at[k, slot], (shift(p, axis, steps), c))
            copy.start()
            copies.append(copy)
            return copy

        def share(k, q, index, src=None):
            if shared is not None:
                held = region(q, k, None)
                copy = remote(held if src is None else src, held, shared[0].at[k, index], shared[1].at[k, index], (p, sibling))
                copy.start()
                siblings.append(copy)

        units = {}
        first_hop, second_hop = {}, {}

        def fan(k, t, q, src=None):
            axis = ring_of[k][1]
            whole = region(q, k, None)
            src = whole if src is None else src
            units[k, t] = q
            second_hop[k, t, 0] = go(k, 4 + 4 * t, src, whole, axis, 1)
            if side == 4:
                second_hop[k, t, 1] = go(k, 5 + 4 * t, src, whole, axis, -1)
            share(k, q, 4 * t, src)

        for k in range(2):
            axis = ring_of[k][0]
            src, whole = origin(p, k, None), region(p, k, None)
            first_hop[k, 0] = go(k, 0, src, whole, axis, 1)
            if side == 4:
                first_hop[k, 1] = go(k, 1, src, whole, axis, -1)
            fan(k, 0, p, src)
        yield
        for k in range(2):
            axis = ring_of[k][0]
            first_hop[k, 0].wait_recv()
            q = shift(p, axis, -1)
            if side == 4:
                part = region(q, k, 0)
                first_hop[k, 2] = go(k, 2, part, part, axis, 1)
            fan(k, 1, q)
        if side == 4:
            for k in range(2):
                axis = ring_of[k][0]
                first_hop[k, 1].wait_recv()
                q = shift(p, axis, 1)
                part = region(q, k, 1)
                first_hop[k, 3] = go(k, 3, part, part, axis, -1)
                fan(k, 2, q)
        yield

        def relay(t):
            for k in range(2):
                axis = ring_of[k][1]
                second_hop[k, t, 0].wait_recv()
                q = shift(units[k, t], axis, -1)
                if side == 4:
                    part = region(q, k, 0)
                    second_hop[k, t, 2] = go(k, 6 + 4 * t, part, part, axis, 1)
                share(k, q, 4 * t + 1)
                if side == 4:
                    second_hop[k, t, 1].wait_recv()
                    q = shift(units[k, t], axis, 1)
                    part = region(q, k, 1)
                    second_hop[k, t, 3] = go(k, 7 + 4 * t, part, part, axis, -1)
                    share(k, q, 4 * t + 2)

        relay(0)
        if side == 4:
            for k in range(2):
                axis = ring_of[k][0]
                first_hop[k, 2].wait_recv()
                first_hop[k, 3].wait_recv()
                fan(k, 3, shift(p, axis, 2))
        yield
        for t in range(1, side):
            relay(t)
        yield
        if side == 4:
            for t in range(side):
                for k in range(2):
                    axis = ring_of[k][1]
                    second_hop[k, t, 2].wait_recv()
                    second_hop[k, t, 3].wait_recv()
                    share(k, shift(units[k, t], axis, 2), 4 * t + 3)
        yield
        for copy in siblings:
            copy.wait_recv()
        for copy in copies + siblings:
            copy.wait_send()
        yield

    keep = pltpu.make_async_copy(piece, lead.at[core, :, pl.ds(pl.multiple_of(p * thin, thin), thin), :], local_sem)
    keep.start()
    lead_gather = plane_gather(lead_region, piece_region, flat_send, flat_recv, (pair_send, pair_recv))
    next(lead_gather)
    next(lead_gather)
    next(lead_gather)

    spread_end(1, first, own)
    vcuts = [remote(pairs.at[d], vv_all.at[lax.rem(p + d, rows)], vcut_send.at[d], vcut_recv, (lax.rem(p + d, rows), c)) for d in range(1, rows)]

    @pl.when(p == c)
    def _():
        for s in range(cols):
            d = lax.rem(s + rows - p, rows)
            lanes = lax.broadcasted_iota(jnp.int32, (BLK, BLK), 1)
            lefts = vu_all[s, 0].astype(jnp.float32)
            rights = pltpu.roll(vu_all[s, 1].astype(jnp.float32), BLK // 2, 1)
            pairs[d] = jnp.where(lanes < BLK // 2, lefts, rights).astype(jnp.bfloat16)
        vv_all[p] = pairs[0]
        for copy in vcuts:
            copy.start()

    next(lead_gather)

    @pl.when(p != c)
    def _():
        vcuts[0].wait_recv()

    pair_gather = plane_gather(pair_region, pair_region, vflat_send, vflat_recv, None)
    next(pair_gather)
    next(pair_gather)
    next(pair_gather)
    next(lead_gather)
    next(pair_gather)
    next(pair_gather)
    next(lead_gather)
    next(pair_gather)
    keep.wait()
    for copy in pending + ring:
        copy.wait_send()

    @pl.when(p == 0)
    def _():
        for copy in cuts:
            copy.wait_send()

    @pl.when(p == c)
    def _():
        for copy in vcuts:
            copy.wait_send()


def exchange(vu, diag_rows):
    rows, cols = lax.axis_size("row"), lax.axis_size("col")
    depth, band, thin = cols // 2, cols // 2 + 1, BLK // rows
    vm = pl.BlockSpec(memory_space=pltpu.VMEM)
    dma = pltpu.SemaphoreType.DMA
    return pl.pallas_call(
        exchange_kernel,
        out_shape=(
            jax.ShapeDtypeStruct((cols, 2, BLK, BLK), jnp.bfloat16),
            jax.ShapeDtypeStruct((rows, BLK, BLK), jnp.bfloat16),
            jax.ShapeDtypeStruct((2, depth * band, BLK, BLK), jnp.float32),
        ),
        in_specs=[vm, vm],
        out_specs=(vm, vm, pl.BlockSpec(memory_space=pl.ANY)),
        scratch_shapes=[
            pltpu.VMEM((band, BLK, BLK), jnp.float32),
            pltpu.VMEM((depth * band, thin, BLK), jnp.float32),
            pltpu.VMEM((rows, BLK, BLK), jnp.bfloat16),
            pltpu.VMEM((cols, BLK, BLK), jnp.bfloat16),
            dma((2, depth)), dma((2, depth)), dma((2, depth)), dma((2, depth)),
            dma((rows,)), dma, dma((depth,)), dma((depth,)),
            dma((2, 20)), dma((2, 20)), dma((2, 16)), dma((2, 16)),
            dma((rows,)), dma, dma((2, 20)), dma((2, 20)), dma,
        ],
        compiler_params=pltpu.CompilerParams(
            collective_id=0, has_side_effects=True, vmem_limit_bytes=40 * 2**20
        ),
    )(vu, diag_rows)


def body(pan_left, pan_right, panel_rank, diag_tiles, col_right, column_rank):
    tile_rows = pan_left.shape[0]
    slab_rows = pan_left.shape[2]
    rank_width = pan_left.shape[3]
    tile_order = diag_tiles.shape[3]
    row_count = lax.axis_size("row")
    col_count = lax.axis_size("col")
    row_index = lax.axis_index("row")
    col_index = lax.axis_index("col")
    col_tiles = tile_rows * row_count // col_count
    columns = lax.broadcasted_iota(jnp.int32, pan_left.shape, 3)
    keep_mask = columns < panel_rank[:, :, None, None]
    zeros_half = jnp.zeros_like(pan_left)
    left_masked = jnp.where(keep_mask, pan_left, zeros_half)
    right_masked = jnp.where(keep_mask, pan_right, zeros_half)
    vu = jnp.concatenate([right_masked, left_masked], axis=3)[:, 0]
    vu_all, vv_all, lead = exchange(vu, diag_tiles[0, 0])
    flat_vu = vu_all.transpose(1, 0, 2, 3).reshape(tile_rows, tile_order, 2 * rank_width)
    right_tiles, left_tiles = flat_vu[:, :, :rank_width], flat_vu[:, :, rank_width:]
    theirs = vv_all.reshape(tile_order, col_tiles, rank_width)
    own_gram = jnp.einsum(
        "anr,ans->ars", right_tiles, right_tiles, preferred_element_type=jnp.float32
    ).astype(jnp.bfloat16)
    products = jnp.einsum(
        "anr,ars->ans", left_tiles, own_gram, preferred_element_type=jnp.float32
    ).astype(jnp.bfloat16)
    product_rows = lax.dynamic_slice_in_dim(products, col_index * slab_rows, slab_rows, 1)
    correction = jnp.einsum(
        "ans,ams->anm", product_rows, left_tiles, preferred_element_type=jnp.float32
    )
    diag_new = diag_tiles - correction[:, None]
    cross_gram = jnp.einsum(
        "anr,nbs->abrs", right_tiles, theirs, preferred_element_type=jnp.float32
    ).astype(jnp.bfloat16)

    narrow_rows = col_right.shape[2]
    rank_ids = lax.broadcasted_iota(jnp.int32, col_right.shape, 2) + col_index * narrow_rows
    tile_ids = lax.broadcasted_iota(jnp.int32, col_right.shape, 0) * row_count + row_index
    keep_right = (rank_ids < column_rank[:, :, None, None]) & (tile_ids >= 1)
    right_kept = jnp.where(keep_right, col_right, jnp.zeros_like(col_right))
    right_side = right_kept.astype(jnp.float32).reshape(-1, tile_order)
    count = right_side.shape[0]
    right_side = jnp.pad(right_side, ((0, -count % 16), (0, 0)))
    place = jnp.stack([row_index, col_index]).astype(jnp.int32)
    solved, lead_part = chol_call(place, lead, right_side, count)
    col_solved = solved.reshape(col_right.shape)

    tile_update = jnp.einsum(
        "anr,abrs->abns", left_tiles, cross_gram, preferred_element_type=jnp.float32
    )
    row_ids = lax.broadcasted_iota(jnp.int32, (tile_rows, col_tiles), 0) * row_count + row_index
    col_ids = lax.broadcasted_iota(jnp.int32, (tile_rows, col_tiles), 1) * col_count + col_index
    lower_mask = (row_ids > col_ids)[:, :, None, None]
    panel_update = jnp.where(lower_mask, tile_update, jnp.zeros_like(tile_update)).astype(
        jnp.bfloat16
    )
    panel_update = panel_update.reshape(tile_rows, 1, col_tiles, 1, tile_order, rank_width)
    return (panel_update, diag_new, lead_part, col_solved)


def solution(mesh):
    placed = (
        P(None, "row", "col", None),
        P(None, "row", "col", None),
        P(None, "row"),
        P(None, "row", "col", None),
        P(None, "row", "col", None),
        P(None, "row"),
    )
    return jax.shard_map(
        body,
        mesh=mesh,
        in_specs=placed,
        out_specs=(
            P(None, "row", None, "col", None, None),
            P(None, "row", "col", None),
            P("row", "col"),
            P(None, "row", "col", None),
        ),
        check_vma=False,
    )
```

```python
import jax, jax.numpy as jnp
from jax import lax
from jax.sharding import PartitionSpec as P
from jax.experimental import pallas as pl
from jax.experimental.pallas import tpu as pltpu

BLK = 128
GRP = 8

def recip(value):
    start = pl.reciprocal(value, approx=True)
    return start * (2.0 - value * start)

def invert_factor(rows):
    count = len(rows)
    shape = (GRP, BLK)
    lanes = lax.broadcasted_iota(jnp.int32, shape, 1)
    subs = lax.broadcasted_iota(jnp.int32, shape, 0)

    def lane(value, index):
        return jnp.broadcast_to(value[:, index : index + 1], shape)

    def line(value, index):
        return jnp.broadcast_to(value[index : index + 1, :], shape)

    kept = [jnp.where(lanes == subs + g * GRP, rows[g], 0.0) for g in range(count)]
    tall = [lax.rsqrt(jnp.broadcast_to(jnp.sum(k, axis=1, keepdims=True), shape)) for k in kept]
    total = kept[0]
    for g in range(1, count):
        total = total + kept[g]
    wide = lax.rsqrt(jnp.broadcast_to(jnp.sum(total, axis=0, keepdims=True), shape))
    rows = [rows[g] * tall[g] * wide for g in range(count)]

    out = []
    edge = [lane(rows[0], k) for k in range(GRP)]
    for g in range(count):
        base = g * GRP
        here = (lanes >= base) & (lanes < base + GRP)
        last = g + 1 == count
        tri = {(i, j): line(edge[j], i) for j in range(GRP) for i in range(j, GRP)}
        cols = {h: [lane(rows[h], base + j) for j in range(GRP)] for h in range(g + 1, count)}
        if not last:
            near = list(cols[g + 1])
            edge = [lane(rows[g + 1], base + GRP + k) for k in range(GRP)]
        pivot = jnp.where(here, jnp.where(lanes - base == subs, 1.0, 0.0), rows[g])
        lines = [line(pivot, j) for j in range(GRP)]
        weight = {}
        pairs = []
        done = jnp.zeros(shape, jnp.float32)
        for j in range(0, GRP, 2):
            a, b, c = tri[j, j], tri[j + 1, j], tri[j + 1, j + 1]
            det = a * c - b * b
            r = recip(det)
            pairs.append((a, b, c, r))
            for i in range(j + 2, GRP):
                x, y = tri[i, j], tri[i, j + 1]
                u, v = c * x - b * y, a * y - b * x
                for k in range(j + 2, i + 1):
                    tri[i, k] = tri[i, k] - r * (u * tri[k, j] + v * tri[k, j + 1])
                weight[i, j], weight[i, j + 1] = u * r, v * r
                lines[i] = lines[i] - (weight[i, j] * lines[j] + weight[i, j + 1] * lines[j + 1])
            if not last:
                u = c * near[j] - b * near[j + 1]
                v = a * near[j + 1] - b * near[j]
                for k in range(GRP):
                    edge[k] = edge[k] - r * (u * line(near[j], k) + v * line(near[j + 1], k))
                for k in range(j + 2, GRP):
                    near[k] = near[k] - r * (u * tri[k, j] + v * tri[k, j + 1])
            root = lax.rsqrt(a)
            done = jnp.where(subs == j, lines[j] * root, done)
            second = (lines[j + 1] - (b * root * root) * lines[j]) * (a * root * lax.rsqrt(det))
            done = jnp.where(subs == j + 1, second, done)
        out.append(jnp.where(lanes <= subs + base, done, 0.0) * wide)
        if not last:
            back = [None] * GRP
            for j in range(GRP - 2, -1, -2):
                a, b, c, r = pairs[j // 2]
                first = r * (c * lines[j] - b * lines[j + 1])
                second = r * (a * lines[j + 1] - b * lines[j])
                for i in range(GRP - 1, j + 1, -1):
                    first = first - weight[i, j] * back[i]
                    second = second - weight[i, j + 1] * back[i]
                back[j], back[j + 1] = first, second
            for h in range(g + 1, count):
                acc = jnp.where(here, 0.0, rows[h])
                for j in range(GRP - 1, -1, -1):
                    acc = acc - cols[h][j] * back[j]
                rows[h] = acc
    return out

NT = (((1,), (1,)), ((), ()))

def halves(value):
    high = value.astype(jnp.bfloat16)
    return high, (value - high.astype(jnp.float32)).astype(jnp.bfloat16)

def mul3(lh, ll, rh, rl):
    def one(x, y):
        return lax.dot_general(x, y, NT, preferred_element_type=jnp.float32)
    return one(lh, rh) + (one(lh, rl) + one(ll, rh))

def chol_kernel(pos_ref, lead_ref, y_ref, x_ref, part_ref, high, low, work, wh, wl):
    order = y_ref.shape[1]
    count = order // BLK
    extra = y_ref.shape[0]
    total = order + extra
    row, col = pos_ref[0], pos_ref[1]

    def block_of(i, k):
        if i < k:
            return jnp.zeros((BLK, BLK), jnp.float32)
        apart = i - k
        source, slot = (i, apart) if 2 * apart <= count else (k, count - apart)
        return lead_ref[source % 2, (source // 2) * (count // 2 + 1) + slot]

    def given(r0, r1, k):
        lo = k * BLK
        parts = [block_of(r // BLK, k) for r in range(r0, min(r1, order), BLK)]
        if r1 > order:
            parts.append(y_ref[max(r0, order) - order:r1 - order, lo:lo + BLK])
        return parts[0] if len(parts) == 1 else jnp.concatenate(parts, axis=0)

    def pair_given(r0, r1, k):
        if k + 1 == count:
            return given(r0, r1, k)
        return jnp.concatenate([given(r0, r1, k), given(r0, r1, k + 1)], axis=1)

    def spans(start, size):
        return [(r, min(r + size, total)) for r in range(start, total, size)]

    for r0, r1 in spans(0, 2 * BLK):
        work[r0:r1, :] = pair_given(r0, r1, 0)
    part_ref[...] = jnp.zeros_like(part_ref)

    def step(k, carry):
        base = pl.multiple_of(k * BLK, BLK)
        side = pl.ds(pl.multiple_of(lax.rem(k, 2) * BLK, BLK), BLK)
        rows = [work[pl.ds(base + g * GRP, GRP), side] for g in range(BLK // GRP)]
        inverse = invert_factor(rows)
        full = jnp.concatenate(inverse, axis=0)
        high_part, low_part = halves(full)
        wh[...] = high_part
        wl[...] = low_part

        for s in range(count):
            @pl.when(k == s)
            def _(s=s):
                lo, hi = s * BLK, s * BLK + BLK
                left = (s % 2) * BLK
                for r0, r1 in spans(lo, 4 * BLK):
                    sh, sl = halves(work[r0:r1, left:left + BLK])
                    panel = mul3(sh, sl, wh[...], wl[...])
                    ph, pl_ = halves(panel)
                    high[r0:r1, lo:hi] = ph
                    low[r0:r1, lo:hi] = pl_
                    work[r0:r1, left:left + BLK] = panel
                x_ref[:, lo:hi] = work[order:order + x_ref.shape[0], left:left + BLK]

                @pl.when(jnp.logical_and(col == s, row >= s))
                def _():
                    block = work[pl.ds(pl.multiple_of(row * BLK, BLK), BLK), left:left + BLK]
                    r = lax.broadcasted_iota(jnp.int32, (BLK, BLK), 0)
                    c = lax.broadcasted_iota(jnp.int32, (BLK, BLK), 1)
                    part_ref[...] = jnp.where((row > s) | (r >= c), block, 0.0)

                if s % 2 == 0 and s + 1 < count:
                    for r0, r1 in spans(hi, 4 * BLK):
                        work[r0:r1, BLK:] = work[r0:r1, BLK:] - mul3(
                            high[r0:r1, lo:hi], low[r0:r1, lo:hi],
                            high[hi:hi + BLK, lo:hi], low[hi:hi + BLK, lo:hi])
                if s % 2 == 1 and s + 1 < count:
                    end = min(hi + 2 * BLK, order)
                    for r0, r1 in spans(hi, 4 * BLK):
                        work[r0:r1, :end - hi] = pair_given(r0, r1, s + 1) - mul3(
                            high[r0:r1, :hi], low[r0:r1, :hi],
                            high[hi:end, :hi], low[hi:end, :hi])
        return carry

    lax.fori_loop(0, count, step, 0)

def chol_call(pos, lead, right, count):
    extra, order = right.shape
    vm = pl.BlockSpec(memory_space=pltpu.VMEM)
    return pl.pallas_call(
        chol_kernel,
        out_shape=(jax.ShapeDtypeStruct((count, order), jnp.float32), jax.ShapeDtypeStruct((BLK, BLK), jnp.float32)),
        in_specs=[pl.BlockSpec(memory_space=pltpu.SMEM), vm, vm],
        out_specs=(vm, vm),
        scratch_shapes=[
            pltpu.VMEM((order + extra, order), jnp.bfloat16),
            pltpu.VMEM((order + extra, order), jnp.bfloat16),
            pltpu.VMEM((order + extra, 2 * BLK), jnp.float32),
            pltpu.VMEM((BLK, BLK), jnp.bfloat16),
            pltpu.VMEM((BLK, BLK), jnp.bfloat16),
        ],
        compiler_params=pltpu.CompilerParams(vmem_limit_bytes=58 * 2**20),
        cost_estimate=pl.CostEstimate(flops=10**11, bytes_accessed=2 * 10**8, transcendentals=0),
    )(pos, lead, right)


def exchange_kernel(
    vu_ref, diag_ref, vu_all, vv_all, lead,
    blocks, piece, pairs, um,
    uv_send, uv_recv, fw_send, fw_recv, cut_send, cut_recv, ring_send, ring_recv,
    flat_send, flat_recv, pair_send, pair_recv, vcut_send, vcut_recv, vflat_send, vflat_recv, local_sem,
):
    rows, cols = cut_send.shape[0], vu_all.shape[0]
    side = {4: 2, 16: 4}[rows]
    depth = cols // 2
    band = cols // 2 + 1
    slots = depth * band
    thin = piece.shape[1]
    p, c = lax.axis_index("row"), lax.axis_index("col")
    z, core = c // 2, lax.rem(c, 2)
    sibling = c + 1 - 2 * core

    def along(d):
        return (p, 2 * lax.rem(z + d, depth) + core)

    def shift(q, axis, steps):
        x, y = q // side, lax.rem(q, side)
        if axis == 0:
            return lax.rem(x + steps + side, side) * side + y
        return x * side + lax.rem(y + steps + side, side)

    def remote(src, dst, send, recv, where):
        return pltpu.make_async_remote_copy(
            src_ref=src, dst_ref=dst, send_sem=send, recv_sem=recv,
            device_id=where, device_id_type=pl.DeviceIdType.MESH,
        )

    barrier = pltpu.get_barrier_semaphore()
    partners = [along(d) for d in range(1, depth)] + [(p, sibling)] + [(lax.rem(p + d, rows), c) for d in range(1, rows)]
    for where in partners:
        pl.semaphore_signal(barrier, inc=1, device_id=where, device_id_type=pl.DeviceIdType.MESH)
    pl.semaphore_wait(barrier, len(partners))

    pending = []

    def spread_start(a):
        first = []
        for d in range(1, depth):
            copy = remote(vu_ref.at[a], vu_all.at[c, a], uv_send.at[a, d], uv_recv.at[a, d], along(d))
            copy.start()
            first.append(copy)
        own = remote(vu_ref.at[a], vu_all.at[c, a], fw_send.at[a, 0], fw_recv.at[a, 0], (p, sibling))
        own.start()
        vu_all[c, a] = vu_ref[a]
        return first, own

    def spread_end(a, first, own):
        later = [own]
        for d in range(1, depth):
            first[d - 1].wait_recv()
            held = vu_all.at[2 * lax.rem(z + depth - d, depth) + core, a]
            copy = remote(held, held, fw_send.at[a, d], fw_recv.at[a, d], (p, sibling))
            copy.start()
            later.append(copy)
        for copy in later:
            copy.wait_recv()
        pending.extend(first + later)

    first, own = spread_start(0)
    spread_end(0, first, own)

    mine_slots = pl.ds(z * band, band)
    cuts = [
        remote(blocks.at[:, pl.ds(d * thin, thin), :], piece.at[mine_slots], cut_send.at[d], cut_recv, (d, c))
        for d in range(1, rows)
    ]

    @pl.when(p == 0)
    def _():
        size = BLK
        r = lax.broadcasted_iota(jnp.int32, (size, size), 0)
        l = lax.broadcasted_iota(jnp.int32, (size, size), 1)
        half = size // 2

        def dots(x, y, dims):
            return lax.dot_general(x, y, (dims, ((), ())), preferred_element_type=jnp.float32)

        gram = jnp.zeros((size, size), jnp.float32)
        for s in range(cols):
            slab = vu_all[s, 0]
            gram = gram + dots(slab, slab, ((0,), (0,)))
        core_w = jnp.where((r < half) & (l < half), gram, 0.0).astype(jnp.bfloat16)
        down = jnp.where(r == l + half, 1.0, 0.0).astype(jnp.bfloat16)
        right = jnp.where(l == r + half, 1.0, 0.0).astype(jnp.bfloat16)
        same = jnp.where((r == l) & (r >= half), 1.0, 0.0)
        low_w = dots(down, core_w, ((1,), (0,)))
        low_w16 = low_w.astype(jnp.bfloat16)
        take_mu = (low_w + same).astype(jnp.bfloat16)
        take_um = (dots(low_w16, right, ((1,), (0,))) + down.astype(jnp.float32)).astype(jnp.bfloat16)
        for s in range(cols):
            um[s] = dots(vu_all[s, 0], take_um, ((1,), (0,))).astype(jnp.bfloat16)
        mine = dots(vu_ref[0], take_mu, ((1,), (0,))).astype(jnp.bfloat16)
        for j in range(band):
            other = lax.rem(c + cols - j, cols)
            fix = dots(mine, um[other], ((1,), (1,)))
            block = diag_ref[:, pl.ds(pl.multiple_of(other * size, size), size)] - 0.5 * fix

            @pl.when(c >= j)
            def _(block=block, j=j):
                blocks[j] = block

            @pl.when(c < j)
            def _(block=block, j=j):
                blocks[j] = block.T
        piece[mine_slots] = blocks[:, :thin, :]
        for copy in cuts:
            copy.start()

    @pl.when(p > 0)
    def _():
        cuts[0].wait_recv()

    ring = []
    for d in range(1, depth):
        copy = remote(piece.at[mine_slots], piece.at[mine_slots], ring_send.at[d], ring_recv.at[d], along(d))
        copy.start()
        ring.append(copy)
    for copy in ring:
        copy.wait_recv()
    first, own = spread_start(1)

    middle, quarter = slots // 2, slots // 4
    edges = [(0, quarter, middle), (middle, middle + quarter, slots)]

    def lead_region(q, k, part):
        lo, mid, hi = edges[k]
        lo, hi = {None: (lo, hi), 0: (lo, mid), 1: (mid, hi)}[part]
        return lead.at[core, pl.ds(lo, hi - lo), pl.ds(pl.multiple_of(q * thin, thin), thin), :]

    def piece_region(q, k, part):
        lo, mid, hi = edges[k]
        return piece.at[pl.ds(lo, hi - lo)]

    def pair_region(q, k, part):
        half = BLK // 2
        lo, size = {None: (0, half), 0: (0, half // 2), 1: (half // 2, half // 2)}[part]
        return vv_all.at[q, pl.ds(k * half + lo, size)]

    def plane_gather(region, origin, send, recv, shared):
        copies, siblings = [], []
        ring_of = [(1 - k, k) for k in range(2)]

        def go(k, slot, src, dst, axis, steps):
            copy = remote(src, dst, send.at[k, slot], recv.at[k, slot], (shift(p, axis, steps), c))
            copy.start()
            copies.append(copy)
            return copy

        def share(k, q, index, src=None):
            if shared is not None:
                held = region(q, k, None)
                copy = remote(held if src is None else src, held, shared[0].at[k, index], shared[1].at[k, index], (p, sibling))
                copy.start()
                siblings.append(copy)

        units = {}
        first_hop, second_hop = {}, {}

        def fan(k, t, q, src=None):
            axis = ring_of[k][1]
            whole = region(q, k, None)
            src = whole if src is None else src
            units[k, t] = q
            second_hop[k, t, 0] = go(k, 4 + 4 * t, src, whole, axis, 1)
            if side == 4:
                second_hop[k, t, 1] = go(k, 5 + 4 * t, src, whole, axis, -1)
            share(k, q, 4 * t, src)

        for k in range(2):
            axis = ring_of[k][0]
            src, whole = origin(p, k, None), region(p, k, None)
            first_hop[k, 0] = go(k, 0, src, whole, axis, 1)
            if side == 4:
                first_hop[k, 1] = go(k, 1, src, whole, axis, -1)
            fan(k, 0, p, src)
        yield
        for k in range(2):
            axis = ring_of[k][0]
            first_hop[k, 0].wait_recv()
            q = shift(p, axis, -1)
            if side == 4:
                part = region(q, k, 0)
                first_hop[k, 2] = go(k, 2, part, part, axis, 1)
            fan(k, 1, q)
        if side == 4:
            for k in range(2):
                axis = ring_of[k][0]
                first_hop[k, 1].wait_recv()
                q = shift(p, axis, 1)
                part = region(q, k, 1)
                first_hop[k, 3] = go(k, 3, part, part, axis, -1)
                fan(k, 2, q)
        yield

        def relay(t):
            for k in range(2):
                axis = ring_of[k][1]
                second_hop[k, t, 0].wait_recv()
                q = shift(units[k, t], axis, -1)
                if side == 4:
                    part = region(q, k, 0)
                    second_hop[k, t, 2] = go(k, 6 + 4 * t, part, part, axis, 1)
                share(k, q, 4 * t + 1)
                if side == 4:
                    second_hop[k, t, 1].wait_recv()
                    q = shift(units[k, t], axis, 1)
                    part = region(q, k, 1)
                    second_hop[k, t, 3] = go(k, 7 + 4 * t, part, part, axis, -1)
                    share(k, q, 4 * t + 2)

        relay(0)
        if side == 4:
            for k in range(2):
                axis = ring_of[k][0]
                first_hop[k, 2].wait_recv()
                first_hop[k, 3].wait_recv()
                fan(k, 3, shift(p, axis, 2))
        yield
        for t in range(1, side):
            relay(t)
        yield
        if side == 4:
            for t in range(side):
                for k in range(2):
                    axis = ring_of[k][1]
                    second_hop[k, t, 2].wait_recv()
                    second_hop[k, t, 3].wait_recv()
                    share(k, shift(units[k, t], axis, 2), 4 * t + 3)
        yield
        for copy in siblings:
            copy.wait_recv()
        for copy in copies + siblings:
            copy.wait_send()
        yield

    keep = pltpu.make_async_copy(piece, lead.at[core, :, pl.ds(pl.multiple_of(p * thin, thin), thin), :], local_sem)
    keep.start()
    lead_gather = plane_gather(lead_region, piece_region, flat_send, flat_recv, (pair_send, pair_recv))
    next(lead_gather)
    next(lead_gather)
    next(lead_gather)

    spread_end(1, first, own)
    vcuts = [remote(pairs.at[d], vv_all.at[lax.rem(p + d, rows)], vcut_send.at[d], vcut_recv, (lax.rem(p + d, rows), c)) for d in range(1, rows)]

    @pl.when(p == c)
    def _():
        for s in range(cols):
            d = lax.rem(s + rows - p, rows)
            lanes = lax.broadcasted_iota(jnp.int32, (BLK, BLK), 1)
            lefts = vu_all[s, 0].astype(jnp.float32)
            rights = pltpu.roll(vu_all[s, 1].astype(jnp.float32), BLK // 2, 1)
            pairs[d] = jnp.where(lanes < BLK // 2, lefts, rights).astype(jnp.bfloat16)
        vv_all[p] = pairs[0]
        for copy in vcuts:
            copy.start()

    next(lead_gather)

    @pl.when(p != c)
    def _():
        vcuts[0].wait_recv()

    pair_gather = plane_gather(pair_region, pair_region, vflat_send, vflat_recv, None)
    next(pair_gather)
    next(pair_gather)
    next(pair_gather)
    next(lead_gather)
    next(pair_gather)
    next(pair_gather)
    next(lead_gather)
    next(pair_gather)
    keep.wait()
    for copy in pending + ring:
        copy.wait_send()

    @pl.when(p == 0)
    def _():
        for copy in cuts:
            copy.wait_send()

    @pl.when(p == c)
    def _():
        for copy in vcuts:
            copy.wait_send()


def exchange(vu, diag_rows):
    rows, cols = lax.axis_size("row"), lax.axis_size("col")
    depth, band, thin = cols // 2, cols // 2 + 1, BLK // rows
    vm = pl.BlockSpec(memory_space=pltpu.VMEM)
    dma = pltpu.SemaphoreType.DMA
    return pl.pallas_call(
        exchange_kernel,
        out_shape=(
            jax.ShapeDtypeStruct((cols, 2, BLK, BLK), jnp.bfloat16),
            jax.ShapeDtypeStruct((rows, BLK, BLK), jnp.bfloat16),
            jax.ShapeDtypeStruct((2, depth * band, BLK, BLK), jnp.float32),
        ),
        in_specs=[vm, vm],
        out_specs=(vm, vm, pl.BlockSpec(memory_space=pl.ANY)),
        scratch_shapes=[
            pltpu.VMEM((band, BLK, BLK), jnp.float32),
            pltpu.VMEM((depth * band, thin, BLK), jnp.float32),
            pltpu.VMEM((rows, BLK, BLK), jnp.bfloat16),
            pltpu.VMEM((cols, BLK, BLK), jnp.bfloat16),
            dma((2, depth)), dma((2, depth)), dma((2, depth)), dma((2, depth)),
            dma((rows,)), dma, dma((depth,)), dma((depth,)),
            dma((2, 20)), dma((2, 20)), dma((2, 16)), dma((2, 16)),
            dma((rows,)), dma, dma((2, 20)), dma((2, 20)), dma,
        ],
        compiler_params=pltpu.CompilerParams(
            collective_id=0, has_side_effects=True, vmem_limit_bytes=40 * 2**20
        ),
    )(vu, diag_rows)


def body(pan_left, pan_right, panel_rank, diag_tiles, col_right, column_rank):
    tile_rows = pan_left.shape[0]
    slab_rows = pan_left.shape[2]
    rank_width = pan_left.shape[3]
    tile_order = diag_tiles.shape[3]
    row_count = lax.axis_size("row")
    col_count = lax.axis_size("col")
    row_index = lax.axis_index("row")
    col_index = lax.axis_index("col")
    col_tiles = tile_rows * row_count // col_count
    columns = lax.broadcasted_iota(jnp.int32, pan_left.shape, 3)
    keep_mask = columns < panel_rank[:, :, None, None]
    zeros_half = jnp.zeros_like(pan_left)
    left_masked = jnp.where(keep_mask, pan_left, zeros_half)
    right_masked = jnp.where(keep_mask, pan_right, zeros_half)
    vu = jnp.concatenate([right_masked, left_masked], axis=3)[:, 0]
    vu_all, vv_all, lead = exchange(vu, diag_tiles[0, 0])
    flat_vu = vu_all.transpose(1, 0, 2, 3).reshape(tile_rows, tile_order, 2 * rank_width)
    right_tiles, left_tiles = flat_vu[:, :, :rank_width], flat_vu[:, :, rank_width:]
    theirs = vv_all.reshape(tile_order, col_tiles, rank_width)
    own_gram = jnp.einsum(
        "anr,ans->ars", right_tiles, right_tiles, preferred_element_type=jnp.float32
    ).astype(jnp.bfloat16)
    products = jnp.einsum(
        "anr,ars->ans", left_tiles, own_gram, preferred_element_type=jnp.float32
    ).astype(jnp.bfloat16)
    product_rows = lax.dynamic_slice_in_dim(products, col_index * slab_rows, slab_rows, 1)
    correction = jnp.einsum(
        "ans,ams->anm", product_rows, left_tiles, preferred_element_type=jnp.float32
    )
    diag_new = diag_tiles - correction[:, None]
    cross_gram = jnp.einsum(
        "anr,nbs->abrs", right_tiles, theirs, preferred_element_type=jnp.float32
    ).astype(jnp.bfloat16)

    narrow_rows = col_right.shape[2]
    rank_ids = lax.broadcasted_iota(jnp.int32, col_right.shape, 2) + col_index * narrow_rows
    tile_ids = lax.broadcasted_iota(jnp.int32, col_right.shape, 0) * row_count + row_index
    keep_right = (rank_ids < column_rank[:, :, None, None]) & (tile_ids >= 1)
    right_kept = jnp.where(keep_right, col_right, jnp.zeros_like(col_right))
    right_side = right_kept.astype(jnp.float32).reshape(-1, tile_order)
    count = right_side.shape[0]
    right_side = jnp.pad(right_side, ((0, -count % 16), (0, 0)))
    place = jnp.stack([row_index, col_index]).astype(jnp.int32)
    solved, lead_part = chol_call(place, lead, right_side, count)
    col_solved = solved.reshape(col_right.shape)

    tile_update = jnp.einsum(
        "anr,abrs->abns", left_tiles, cross_gram, preferred_element_type=jnp.float32
    )
    row_ids = lax.broadcasted_iota(jnp.int32, (tile_rows, col_tiles), 0) * row_count + row_index
    col_ids = lax.broadcasted_iota(jnp.int32, (tile_rows, col_tiles), 1) * col_count + col_index
    lower_mask = (row_ids > col_ids)[:, :, None, None]
    panel_update = jnp.where(lower_mask, tile_update, jnp.zeros_like(tile_update)).astype(
        jnp.bfloat16
    )
    panel_update = panel_update.reshape(tile_rows, 1, col_tiles, 1, tile_order, rank_width)
    return (panel_update, diag_new, lead_part, col_solved)


def solution(mesh):
    placed = (
        P(None, "row", "col", None),
        P(None, "row", "col", None),
        P(None, "row"),
        P(None, "row", "col", None),
        P(None, "row", "col", None),
        P(None, "row"),
    )
    return jax.shard_map(
        body,
        mesh=mesh,
        in_specs=placed,
        out_specs=(
            P(None, "row", None, "col", None, None),
            P(None, "row", "col", None),
            P("row", "col"),
            P(None, "row", "col", None),
        ),
        check_vma=False,
    )
```

```python
import jax, jax.numpy as jnp
from jax import lax
from jax.sharding import PartitionSpec as P
from jax.experimental import pallas as pl
from jax.experimental.pallas import tpu as pltpu

BLK = 128
GRP = 8

def recip(value):
    start = pl.reciprocal(value, approx=True)
    return start * (2.0 - value * start)

def invert_factor(rows):
    count = len(rows)
    shape = (GRP, BLK)
    lanes = lax.broadcasted_iota(jnp.int32, shape, 1)
    subs = lax.broadcasted_iota(jnp.int32, shape, 0)

    def lane(value, index):
        return jnp.broadcast_to(value[:, index : index + 1], shape)

    def line(value, index):
        return jnp.broadcast_to(value[index : index + 1, :], shape)

    kept = [jnp.where(lanes == subs + g * GRP, rows[g], 0.0) for g in range(count)]
    tall = [lax.rsqrt(jnp.broadcast_to(jnp.sum(k, axis=1, keepdims=True), shape)) for k in kept]
    total = kept[0]
    for g in range(1, count):
        total = total + kept[g]
    wide = lax.rsqrt(jnp.broadcast_to(jnp.sum(total, axis=0, keepdims=True), shape))
    rows = [rows[g] * tall[g] * wide for g in range(count)]

    out = []
    edge = [lane(rows[0], k) for k in range(GRP)]
    for g in range(count):
        base = g * GRP
        here = (lanes >= base) & (lanes < base + GRP)
        last = g + 1 == count
        tri = {(i, j): line(edge[j], i) for j in range(GRP) for i in range(j, GRP)}
        cols = {h: [lane(rows[h], base + j) for j in range(GRP)] for h in range(g + 1, count)}
        if not last:
            near = list(cols[g + 1])
            edge = [lane(rows[g + 1], base + GRP + k) for k in range(GRP)]
        pivot = jnp.where(here, jnp.where(lanes - base == subs, 1.0, 0.0), rows[g])
        lines = [line(pivot, j) for j in range(GRP)]
        weight = {}
        pairs = []
        done = jnp.zeros(shape, jnp.float32)
        for j in range(0, GRP, 2):
            a, b, c = tri[j, j], tri[j + 1, j], tri[j + 1, j + 1]
            det = a * c - b * b
            r = recip(det)
            pairs.append((a, b, c, r))
            for i in range(j + 2, GRP):
                x, y = tri[i, j], tri[i, j + 1]
                u, v = c * x - b * y, a * y - b * x
                for k in range(j + 2, i + 1):
                    tri[i, k] = tri[i, k] - r * (u * tri[k, j] + v * tri[k, j + 1])
                weight[i, j], weight[i, j + 1] = u * r, v * r
                lines[i] = lines[i] - (weight[i, j] * lines[j] + weight[i, j + 1] * lines[j + 1])
            if not last:
                u = c * near[j] - b * near[j + 1]
                v = a * near[j + 1] - b * near[j]
                for k in range(GRP):
                    edge[k] = edge[k] - r * (u * line(near[j], k) + v * line(near[j + 1], k))
                for k in range(j + 2, GRP):
                    near[k] = near[k] - r * (u * tri[k, j] + v * tri[k, j + 1])
            root = lax.rsqrt(a)
            done = jnp.where(subs == j, lines[j] * root, done)
            second = (lines[j + 1] - (b * root * root) * lines[j]) * (a * root * lax.rsqrt(det))
            done = jnp.where(subs == j + 1, second, done)
        out.append(jnp.where(lanes <= subs + base, done, 0.0) * wide)
        if not last:
            back = [None] * GRP
            for j in range(GRP - 2, -1, -2):
                a, b, c, r = pairs[j // 2]
                first = r * (c * lines[j] - b * lines[j + 1])
                second = r * (a * lines[j + 1] - b * lines[j])
                for i in range(GRP - 1, j + 1, -1):
                    first = first - weight[i, j] * back[i]
                    second = second - weight[i, j + 1] * back[i]
                back[j], back[j + 1] = first, second
            for h in range(g + 1, count):
                acc = jnp.where(here, 0.0, rows[h])
                for j in range(GRP - 1, -1, -1):
                    acc = acc - cols[h][j] * back[j]
                rows[h] = acc
    return out

NT = (((1,), (1,)), ((), ()))

def halves(value):
    high = value.astype(jnp.bfloat16)
    return high, (value - high.astype(jnp.float32)).astype(jnp.bfloat16)

def mul3(lh, ll, rh, rl):
    def one(x, y):
        return lax.dot_general(x, y, NT, preferred_element_type=jnp.float32)
    return one(lh, rh) + (one(lh, rl) + one(ll, rh))

MESH = pl.DeviceIdType.MESH


def lead_place(i, k, count):
    first = early_count(count)
    if k < first:
        return 0, i, k
    apart, ring = i - k, count - first
    source, slot = (i, apart) if 2 * apart <= ring else (k, ring - apart)
    return 1, source, slot


def early_count(count):
    return max(2, count // 4)


def update_kernel(
    vu_ref, diag_ref, y_ref,
    vu_all, vv_all, x_ref, part_ref,
    lead_a, lead_b, blocks_a, blocks_b, piece_a, piece_b, pairs, um, own_mu, high, low, work, wh, wl,
    uv_send, uv_recv, fw_send, fw_recv, cut_send, cut_recv, ring_send, ring_recv,
    flat_send, flat_recv, pair_send, pair_recv, vcut_send, vcut_recv, vflat_send, vflat_recv, local_sem,
):
    rows, cols = cut_send.shape[1], vu_all.shape[0]
    side = {4: 2, 16: 4}[rows]
    depth = cols // 2
    early = early_count(cols)
    late = cols - early
    thin = piece_a.shape[1]
    p, c = lax.axis_index("row"), lax.axis_index("col")
    z, core = c // 2, lax.rem(c, 2)
    sibling = c + 1 - 2 * core

    order = y_ref.shape[1]
    count = cols
    total = order + y_ref.shape[0]

    def along(d):
        return (p, 2 * lax.rem(z + d, depth) + core)

    def shift(q, axis, steps):
        x, y = q // side, lax.rem(q, side)
        if axis == 0:
            return lax.rem(x + steps + side, side) * side + y
        return x * side + lax.rem(y + steps + side, side)

    def remote(src, dst, send, recv, where):
        return pltpu.make_async_remote_copy(
            src_ref=src, dst_ref=dst, send_sem=send, recv_sem=recv, device_id=where, device_id_type=MESH
        )

    def start_all(copies):
        for copy in copies:
            copy.start()

    barrier = pltpu.get_barrier_semaphore()
    partners = [along(d) for d in range(1, depth)] + [(p, sibling)] + [(lax.rem(p + d, rows), c) for d in range(1, rows)]
    for where in partners:
        pl.semaphore_signal(barrier, inc=1, device_id=where, device_id_type=MESH)
    pl.semaphore_wait(barrier, len(partners))

    spreads = []
    for a in range(2):
        first = [
            remote(vu_ref.at[a], vu_all.at[c, a], uv_send.at[a, d], uv_recv.at[a, d], along(d)) for d in range(1, depth)
        ]
        held = [vu_all.at[2 * lax.rem(z + depth - d, depth) + core, a] for d in range(depth)]
        later = [remote(vu_ref.at[a], vu_all.at[c, a], fw_send.at[a, 0], fw_recv.at[a, 0], (p, sibling))] + [
            remote(held[d], held[d], fw_send.at[a, d], fw_recv.at[a, d], (p, sibling)) for d in range(1, depth)
        ]
        spreads.append((first, later))

    def spread_start(a):
        first, later = spreads[a]
        start_all(first)
        later[0].start()
        vu_all[c, a] = vu_ref[a]

    def spread_pass(a):
        first, later = spreads[a]
        for one, two in zip(first, later[1:]):
            one.wait_recv()
            two.start()

    def spread_end(a):
        for copy in spreads[a][1]:
            copy.wait_recv()

    phases = []
    for f, (blocks, piece) in enumerate(((blocks_a, piece_a), (blocks_b, piece_b))):
        wide = blocks.shape[0]
        mine = piece.at[pl.ds(z * wide, wide)]
        cuts = [
            remote(blocks.at[:, pl.ds(d * thin, thin), :], mine, cut_send.at[f, d], cut_recv.at[f], (d, c))
            for d in range(1, rows)
        ]
        ring = [remote(mine, mine, ring_send.at[f, d], ring_recv.at[f, d], along(d)) for d in range(1, depth)]
        phases.append((cuts, ring, mine))

    def plane_gather(region, origin, send, recv, shared):
        hops, shares = {}, {}
        units = {}

        def add(k, slot, src, dst, axis, steps):
            hops[k, slot] = remote(src, dst, send.at[k, slot], recv.at[k, slot], (shift(p, axis, steps), c))

        def share(k, index, q, src=None):
            if shared is not None:
                held = region(q, k, None)
                shares[k, index] = remote(
                    held if src is None else src, held, shared[0].at[k, index], shared[1].at[k, index], (p, sibling)
                )

        for k in range(2):
            one, two = 1 - k, k
            src, whole = origin(k), region(p, k, None)
            add(k, 0, src, whole, one, 1)
            if side == 4:
                add(k, 1, src, whole, one, -1)
                back, ahead = region(shift(p, one, -1), k, 0), region(shift(p, one, 1), k, 1)
                add(k, 2, back, back, one, 1)
                add(k, 3, ahead, ahead, one, -1)
            steps = (0, -1, 1, 2)[:side]
            for t, step in enumerate(steps):
                q = shift(p, one, step) if step else p
                whole = region(q, k, None)
                src = origin(k) if t == 0 else whole
                add(k, 4 + 4 * t, src, whole, two, 1)
                share(k, 4 * t, q, src)
                share(k, 4 * t + 1, shift(q, two, -1))
                if side == 4:
                    add(k, 5 + 4 * t, src, whole, two, -1)
                    back, ahead = region(shift(q, two, -1), k, 0), region(shift(q, two, 1), k, 1)
                    add(k, 6 + 4 * t, back, back, two, 1)
                    add(k, 7 + 4 * t, ahead, ahead, two, -1)
                    share(k, 4 * t + 2, shift(q, two, 1))
                    share(k, 4 * t + 3, shift(q, two, 2))

        def go(k, slot):
            if (k, slot) in hops:
                hops[k, slot].start()

        def arrived(k, slot):
            if (k, slot) in hops:
                hops[k, slot].wait_recv()

        def hand(k, index):
            if (k, index) in shares:
                shares[k, index].start()

        def fan(k, t):
            go(k, 4 + 4 * t)
            go(k, 5 + 4 * t)
            hand(k, 4 * t)

        def relay(t):
            for k in range(2):
                arrived(k, 4 + 4 * t)
                go(k, 6 + 4 * t)
                hand(k, 4 * t + 1)
                arrived(k, 5 + 4 * t)
                go(k, 7 + 4 * t)
                hand(k, 4 * t + 2)

        def stage(number):
            if number == 0:
                for k in range(2):
                    go(k, 0)
                    go(k, 1)
                    fan(k, 0)
            if number == 1:
                for k in range(2):
                    arrived(k, 0)
                    go(k, 2)
                    fan(k, 1)
                if side == 4:
                    for k in range(2):
                        arrived(k, 1)
                        go(k, 3)
                        fan(k, 2)
            if number == 2:
                relay(0)
                if side == 4:
                    for k in range(2):
                        arrived(k, 2)
                        arrived(k, 3)
                        fan(k, 3)
            if number == 3:
                for t in range(1, side):
                    relay(t)
            if number == 4 and side == 4:
                for t in range(side):
                    for k in range(2):
                        arrived(k, 6 + 4 * t)
                        arrived(k, 7 + 4 * t)
                        hand(k, 4 * t + 3)
            if number == 5:
                for copy in shares.values():
                    copy.wait_recv()
            if number == 6:
                for copy in list(hops.values()) + list(shares.values()):
                    copy.wait_send()

        return stage

    def lead_stages(f, lead, piece, skip):
        slots = lead.shape[1]
        middle, quarter = slots // 2, slots // 4
        edges = [(0, quarter, middle), (middle, middle + quarter, slots)]

        def region(q, k, part):
            lo, mid, hi = edges[k]
            lo, hi = {None: (lo, hi), 0: (lo, mid), 1: (mid, hi)}[part]
            return lead.at[core, pl.ds(lo, hi - lo), pl.ds(pl.multiple_of(q * thin, thin), thin), :]

        def origin(k):
            lo, mid, hi = edges[k]
            return piece.at[pl.ds(skip + lo, hi - lo)]

        stage = plane_gather(region, origin, flat_send.at[f], flat_recv.at[f], (pair_send.at[f], pair_recv.at[f]))
        keep = pltpu.make_async_copy(
            piece.at[pl.ds(skip, slots)],
            lead.at[core, :, pl.ds(pl.multiple_of(p * thin, thin), thin), :],
            local_sem.at[f],
        )
        return stage, keep

    skip_b = (early // 2) * blocks_b.shape[0]
    stage_a, keep_a = lead_stages(0, lead_a, piece_a, 0)
    stage_b, keep_b = lead_stages(1, lead_b, piece_b, skip_b)

    def pair_region(q, k, part):
        half = BLK // 2
        lo, size = {None: (0, half), 0: (0, half // 2), 1: (half // 2, half // 2)}[part]
        return vv_all.at[q, pl.ds(k * half + lo, size)]

    stage_v = plane_gather(pair_region, lambda k: pair_region(p, k, None), vflat_send, vflat_recv, None)
    vcuts = [
        remote(pairs.at[d], vv_all.at[lax.rem(p + d, rows)], vcut_send.at[d], vcut_recv, (lax.rem(p + d, rows), c))
        for d in range(1, rows)
    ]
    turns = [lax.rem(s + rows - p, rows) for s in range(cols)]

    def lead_block(other):
        fix = lax.dot_general(own_mu[...], um[other], NT, preferred_element_type=jnp.float32)
        return diag_ref[:, pl.ds(pl.multiple_of(other * BLK, BLK), BLK)] - 0.5 * fix

    spread_start(0)
    spread_pass(0)
    spread_end(0)

    @pl.when(p == 0)
    def _():
        size = BLK
        r = lax.broadcasted_iota(jnp.int32, (size, size), 0)
        l = lax.broadcasted_iota(jnp.int32, (size, size), 1)
        half = size // 2

        def dots(x, y, dims):
            return lax.dot_general(x, y, (dims, ((), ())), preferred_element_type=jnp.float32)

        gram = jnp.zeros((size, size), jnp.float32)
        for s in range(cols):
            slab = vu_all[s, 0]
            gram = gram + dots(slab, slab, ((0,), (0,)))
        core_w = jnp.where((r < half) & (l < half), gram, 0.0).astype(jnp.bfloat16)
        down = jnp.where(r == l + half, 1.0, 0.0).astype(jnp.bfloat16)
        right = jnp.where(l == r + half, 1.0, 0.0).astype(jnp.bfloat16)
        same = jnp.where((r == l) & (r >= half), 1.0, 0.0)
        low_w = dots(down, core_w, ((1,), (0,)))
        low_w16 = low_w.astype(jnp.bfloat16)
        take_mu = (low_w + same).astype(jnp.bfloat16)
        take_um = (dots(low_w16, right, ((1,), (0,))) + down.astype(jnp.float32)).astype(jnp.bfloat16)
        for s in range(cols):
            um[s] = dots(vu_all[s, 0], take_um, ((1,), (0,))).astype(jnp.bfloat16)
        own_mu[...] = dots(vu_ref[0], take_mu, ((1,), (0,))).astype(jnp.bfloat16)
        for j in range(early):
            blocks_a[j] = lead_block(j)
        phases[0][2][...] = blocks_a[:, :thin, :]
        start_all(phases[0][0])

    @pl.when(p > 0)
    def _():
        phases[0][0][0].wait_recv()

    start_all(phases[0][1])

    @pl.when(p == 0)
    def _():
        for j in range(late // 2 + 1):
            other = early + lax.rem(c - early - j + 2 * late, late)
            block = lead_block(other)

            @pl.when(c >= other)
            def _(block=block, j=j):
                blocks_b[j] = block

            @pl.when(c < other)
            def _(block=block, j=j):
                blocks_b[j] = block.T
        phases[1][2][...] = blocks_b[:, :thin, :]
        start_all(phases[1][0])

    for copy in phases[0][1]:
        copy.wait_recv()
    keep_a.start()
    stage_a(0)

    @pl.when(p > 0)
    def _():
        phases[1][0][0].wait_recv()

    stage_a(1)
    start_all(phases[1][1])
    stage_a(2)
    stage_a(3)
    stage_a(4)
    for copy in phases[1][1]:
        copy.wait_recv()
    keep_b.start()
    stage_b(0)
    spread_start(1)
    keep_a.wait()
    stage_a(5)

    def build_pairs():
        @pl.when(p == c)
        def _():
            for s in range(cols):
                lanes = lax.broadcasted_iota(jnp.int32, (BLK, BLK), 1)
                lefts = vu_all[s, 0].astype(jnp.float32)
                rights = pltpu.roll(vu_all[s, 1].astype(jnp.float32), BLK // 2, 1)
                pairs[turns[s]] = jnp.where(lanes < BLK // 2, lefts, rights).astype(jnp.bfloat16)
            vv_all[p] = pairs[0]
            start_all(vcuts)

    def take_pairs():
        @pl.when(p != c)
        def _():
            vcuts[0].wait_recv()

    def errands(s):
        if s < early:
            stage_b(s + 1)
        if s == early - 1:
            for number in range(early + 1, 6):
                stage_b(number)
            keep_b.wait()
        if count == 16:
            plan = {4: [lambda: spread_pass(1)], 5: [lambda: spread_end(1), build_pairs], 6: [take_pairs, lambda: stage_v(0)],
                    7: [lambda: stage_v(1)], 8: [lambda: stage_v(2)], 9: [lambda: stage_v(3)], 10: [lambda: stage_v(4)]}
        else:
            plan = {3: [lambda: spread_pass(1), lambda: spread_end(1), build_pairs, take_pairs] + [lambda n=n: stage_v(n) for n in range(5)]}
        for act in plan.get(s, []):
            act()

    def block_of(i, k):
        if i < k:
            return jnp.zeros((BLK, BLK), jnp.float32)
        phase, source, slot = lead_place(i, k, count)
        if phase == 0:
            return lead_a[source % 2, (source // 2) * early + slot]
        return lead_b[source % 2, (source // 2 - early // 2) * (late // 2 + 1) + slot]

    def given(r0, r1, k):
        lo = k * BLK
        parts = [block_of(r // BLK, k) for r in range(r0, min(r1, order), BLK)]
        if r1 > order:
            parts.append(y_ref[max(r0, order) - order:r1 - order, lo:lo + BLK])
        return parts[0] if len(parts) == 1 else jnp.concatenate(parts, axis=0)

    def pair_given(r0, r1, k):
        return jnp.concatenate([given(r0, r1, k), given(r0, r1, k + 1)], axis=1)

    def spans(start, size):
        return [(r, min(r + size, total)) for r in range(start, total, size)]

    for r0, r1 in spans(0, 2 * BLK):
        work[r0:r1, :] = pair_given(r0, r1, 0)
    part_ref[...] = jnp.zeros_like(part_ref)

    def step(k, carry):
        base = pl.multiple_of(k * BLK, BLK)
        flank = pl.ds(pl.multiple_of(lax.rem(k, 2) * BLK, BLK), BLK)
        inverse = invert_factor([work[pl.ds(base + g * GRP, GRP), flank] for g in range(BLK // GRP)])
        high_part, low_part = halves(jnp.concatenate(inverse, axis=0))
        wh[...] = high_part
        wl[...] = low_part

        for s in range(count):
            @pl.when(k == s)
            def _(s=s):
                lo, hi = s * BLK, s * BLK + BLK
                left = (s % 2) * BLK
                errands(s)
                for r0, r1 in spans(lo, 4 * BLK):
                    sh, sl = halves(work[r0:r1, left:left + BLK])
                    panel = mul3(sh, sl, wh[...], wl[...])
                    ph, pl_ = halves(panel)
                    high[r0:r1, lo:hi] = ph
                    low[r0:r1, lo:hi] = pl_
                    work[r0:r1, left:left + BLK] = panel
                x_ref[:, lo:hi] = work[order:order + x_ref.shape[0], left:left + BLK]

                @pl.when(jnp.logical_and(c == s, p >= s))
                def _():
                    block = work[pl.ds(pl.multiple_of(p * BLK, BLK), BLK), left:left + BLK]
                    r = lax.broadcasted_iota(jnp.int32, (BLK, BLK), 0)
                    l = lax.broadcasted_iota(jnp.int32, (BLK, BLK), 1)
                    part_ref[...] = jnp.where((p > s) | (r >= l), block, 0.0)

                if s % 2 == 0 and s + 1 < count:
                    for r0, r1 in spans(hi, 4 * BLK):
                        work[r0:r1, BLK:] = work[r0:r1, BLK:] - mul3(
                            high[r0:r1, lo:hi], low[r0:r1, lo:hi],
                            high[hi:hi + BLK, lo:hi], low[hi:hi + BLK, lo:hi])
                if s % 2 == 1 and s + 1 < count:
                    end = hi + 2 * BLK
                    for r0, r1 in spans(hi, 4 * BLK):
                        work[r0:r1, :] = pair_given(r0, r1, s + 1) - mul3(
                            high[r0:r1, :hi], low[r0:r1, :hi],
                            high[hi:end, :hi], low[hi:end, :hi])
        return carry

    lax.fori_loop(0, count, step, 0)

    stage_a(6)
    stage_b(6)
    stage_v(6)
    for first, later in spreads:
        for copy in first + later:
            copy.wait_send()
    for cuts, ring, mine in phases:
        for copy in ring:
            copy.wait_send()

    @pl.when(p == 0)
    def _():
        for cuts, ring, mine in phases:
            for copy in cuts:
                copy.wait_send()

    @pl.when(p == c)
    def _():
        for copy in vcuts:
            copy.wait_send()


def update_call(vu, diag_rows, right, narrow):
    rows, cols = lax.axis_size("row"), lax.axis_size("col")
    depth, thin = cols // 2, BLK // rows
    extra, order = right.shape
    early = early_count(cols)
    late = (cols - early) // 2 + 1
    vm = pl.BlockSpec(memory_space=pltpu.VMEM)
    dma = pltpu.SemaphoreType.DMA
    wide, half = jnp.float32, jnp.bfloat16
    return pl.pallas_call(
        update_kernel,
        out_shape=(
            jax.ShapeDtypeStruct((cols, 2, BLK, BLK), half),
            jax.ShapeDtypeStruct((rows, BLK, BLK), half),
            jax.ShapeDtypeStruct((narrow, order), wide),
            jax.ShapeDtypeStruct((BLK, BLK), wide),
        ),
        in_specs=[vm, vm, vm],
        out_specs=(vm, vm, vm, vm),
        scratch_shapes=[
            pltpu.VMEM((2, depth * early, BLK, BLK), wide),
            pltpu.VMEM((2, (depth - early // 2) * late, BLK, BLK), wide),
            pltpu.VMEM((early, BLK, BLK), wide),
            pltpu.VMEM((late, BLK, BLK), wide),
            pltpu.VMEM((depth * early, thin, BLK), wide),
            pltpu.VMEM((depth * late, thin, BLK), wide),
            pltpu.VMEM((rows, BLK, BLK), half),
            pltpu.VMEM((cols, BLK, BLK), half),
            pltpu.VMEM((BLK, BLK), half),
            pltpu.VMEM((order + extra, order), half),
            pltpu.VMEM((order + extra, order), half),
            pltpu.VMEM((order + extra, 2 * BLK), wide),
            pltpu.VMEM((BLK, BLK), half),
            pltpu.VMEM((BLK, BLK), half),
            dma((2, depth)), dma((2, depth)), dma((2, depth)), dma((2, depth)),
            dma((2, rows)), dma((2,)), dma((2, depth)), dma((2, depth)),
            dma((2, 2, 20)), dma((2, 2, 20)), dma((2, 2, 16)), dma((2, 2, 16)),
            dma((rows,)), dma, dma((2, 20)), dma((2, 20)), dma((2,)),
        ],
        compiler_params=pltpu.CompilerParams(
            collective_id=0, has_side_effects=True, vmem_limit_bytes=56 * 2**20
        ),
        cost_estimate=pl.CostEstimate(flops=10**11, bytes_accessed=2 * 10**7, transcendentals=0),
    )(vu, diag_rows, right)


def body(pan_left, pan_right, panel_rank, diag_tiles, col_right, column_rank):
    tile_rows = pan_left.shape[0]
    slab_rows = pan_left.shape[2]
    rank_width = pan_left.shape[3]
    tile_order = diag_tiles.shape[3]
    row_count = lax.axis_size("row")
    col_count = lax.axis_size("col")
    row_index = lax.axis_index("row")
    col_index = lax.axis_index("col")
    col_tiles = tile_rows * row_count // col_count
    columns = lax.broadcasted_iota(jnp.int32, pan_left.shape, 3)
    keep_mask = columns < panel_rank[:, :, None, None]
    zeros_half = jnp.zeros_like(pan_left)
    left_masked = jnp.where(keep_mask, pan_left, zeros_half)
    right_masked = jnp.where(keep_mask, pan_right, zeros_half)
    vu = jnp.concatenate([right_masked, left_masked], axis=3)[:, 0]
    narrow_rows = col_right.shape[2]
    rank_ids = lax.broadcasted_iota(jnp.int32, col_right.shape, 2) + col_index * narrow_rows
    tile_ids = lax.broadcasted_iota(jnp.int32, col_right.shape, 0) * row_count + row_index
    keep_right = (rank_ids < column_rank[:, :, None, None]) & (tile_ids >= 1)
    right_kept = jnp.where(keep_right, col_right, jnp.zeros_like(col_right))
    right_side = right_kept.astype(jnp.float32).reshape(-1, tile_order)
    count = right_side.shape[0]
    right_side = jnp.pad(right_side, ((0, -count % 16), (0, 0)))
    vu_all, vv_all, solved, lead_part = update_call(vu, diag_tiles[0, 0], right_side, count)
    flat_vu = vu_all.transpose(1, 0, 2, 3).reshape(tile_rows, tile_order, 2 * rank_width)
    right_tiles, left_tiles = flat_vu[:, :, :rank_width], flat_vu[:, :, rank_width:]
    theirs = vv_all.reshape(tile_order, col_tiles, rank_width)
    own_gram = jnp.einsum(
        "anr,ans->ars", right_tiles, right_tiles, preferred_element_type=jnp.float32
    ).astype(jnp.bfloat16)
    products = jnp.einsum(
        "anr,ars->ans", left_tiles, own_gram, preferred_element_type=jnp.float32
    ).astype(jnp.bfloat16)
    product_rows = lax.dynamic_slice_in_dim(products, col_index * slab_rows, slab_rows, 1)
    correction = jnp.einsum(
        "ans,ams->anm", product_rows, left_tiles, preferred_element_type=jnp.float32
    )
    diag_new = diag_tiles - correction[:, None]
    cross_gram = jnp.einsum(
        "anr,nbs->abrs", right_tiles, theirs, preferred_element_type=jnp.float32
    ).astype(jnp.bfloat16)

    col_solved = solved.reshape(col_right.shape)

    tile_update = jnp.einsum(
        "anr,abrs->abns", left_tiles, cross_gram, preferred_element_type=jnp.float32
    )
    row_ids = lax.broadcasted_iota(jnp.int32, (tile_rows, col_tiles), 0) * row_count + row_index
    col_ids = lax.broadcasted_iota(jnp.int32, (tile_rows, col_tiles), 1) * col_count + col_index
    lower_mask = (row_ids > col_ids)[:, :, None, None]
    panel_update = jnp.where(lower_mask, tile_update, jnp.zeros_like(tile_update)).astype(
        jnp.bfloat16
    )
    panel_update = panel_update.reshape(tile_rows, 1, col_tiles, 1, tile_order, rank_width)
    return (panel_update, diag_new, lead_part, col_solved)


def solution(mesh):
    placed = (
        P(None, "row", "col", None),
        P(None, "row", "col", None),
        P(None, "row"),
        P(None, "row", "col", None),
        P(None, "row", "col", None),
        P(None, "row"),
    )
    return jax.shard_map(
        body,
        mesh=mesh,
        in_specs=placed,
        out_specs=(
            P(None, "row", None, "col", None, None),
            P(None, "row", "col", None),
            P("row", "col"),
            P(None, "row", "col", None),
        ),
        check_vma=False,
    )
```

```python
import jax, jax.numpy as jnp
from jax import lax
from jax.sharding import PartitionSpec as P
from jax.experimental import pallas as pl
from jax.experimental.pallas import tpu as pltpu

BLK = 128
GRP = 8

def recip(value):
    start = pl.reciprocal(value, approx=True)
    return start * (2.0 - value * start)

def invert_factor(rows):
    count = len(rows)
    shape = (GRP, BLK)
    lanes = lax.broadcasted_iota(jnp.int32, shape, 1)
    subs = lax.broadcasted_iota(jnp.int32, shape, 0)

    def lane(value, index):
        return jnp.broadcast_to(value[:, index : index + 1], shape)

    def line(value, index):
        return jnp.broadcast_to(value[index : index + 1, :], shape)

    kept = [jnp.where(lanes == subs + g * GRP, rows[g], 0.0) for g in range(count)]
    tall = [lax.rsqrt(jnp.broadcast_to(jnp.sum(k, axis=1, keepdims=True), shape)) for k in kept]
    total = kept[0]
    for g in range(1, count):
        total = total + kept[g]
    wide = lax.rsqrt(jnp.broadcast_to(jnp.sum(total, axis=0, keepdims=True), shape))
    rows = [rows[g] * tall[g] * wide for g in range(count)]

    out = []
    edge = [lane(rows[0], k) for k in range(GRP)]
    for g in range(count):
        base = g * GRP
        here = (lanes >= base) & (lanes < base + GRP)
        last = g + 1 == count
        tri = {(i, j): line(edge[j], i) for j in range(GRP) for i in range(j, GRP)}
        cols = {h: [lane(rows[h], base + j) for j in range(GRP)] for h in range(g + 1, count)}
        if not last:
            near = list(cols[g + 1])
            edge = [lane(rows[g + 1], base + GRP + k) for k in range(GRP)]
        pivot = jnp.where(here, jnp.where(lanes - base == subs, 1.0, 0.0), rows[g])
        lines = [line(pivot, j) for j in range(GRP)]
        weight = {}
        pairs = []
        done = jnp.zeros(shape, jnp.float32)
        for j in range(0, GRP, 2):
            a, b, c = tri[j, j], tri[j + 1, j], tri[j + 1, j + 1]
            det = a * c - b * b
            r = recip(det)
            pairs.append((a, b, c, r))
            for i in range(j + 2, GRP):
                x, y = tri[i, j], tri[i, j + 1]
                u, v = c * x - b * y, a * y - b * x
                for k in range(j + 2, i + 1):
                    tri[i, k] = tri[i, k] - r * (u * tri[k, j] + v * tri[k, j + 1])
                weight[i, j], weight[i, j + 1] = u * r, v * r
                lines[i] = lines[i] - (weight[i, j] * lines[j] + weight[i, j + 1] * lines[j + 1])
            if not last:
                u = c * near[j] - b * near[j + 1]
                v = a * near[j + 1] - b * near[j]
                for k in range(GRP):
                    edge[k] = edge[k] - r * (u * line(near[j], k) + v * line(near[j + 1], k))
                for k in range(j + 2, GRP):
                    near[k] = near[k] - r * (u * tri[k, j] + v * tri[k, j + 1])
            root = lax.rsqrt(a)
            done = jnp.where(subs == j, lines[j] * root, done)
            second = (lines[j + 1] - (b * root * root) * lines[j]) * (a * root * lax.rsqrt(det))
            done = jnp.where(subs == j + 1, second, done)
        out.append(jnp.where(lanes <= subs + base, done, 0.0) * wide)
        if not last:
            back = [None] * GRP
            for j in range(GRP - 2, -1, -2):
                a, b, c, r = pairs[j // 2]
                first = r * (c * lines[j] - b * lines[j + 1])
                second = r * (a * lines[j + 1] - b * lines[j])
                for i in range(GRP - 1, j + 1, -1):
                    first = first - weight[i, j] * back[i]
                    second = second - weight[i, j + 1] * back[i]
                back[j], back[j + 1] = first, second
            for h in range(g + 1, count):
                acc = jnp.where(here, 0.0, rows[h])
                for j in range(GRP - 1, -1, -1):
                    acc = acc - cols[h][j] * back[j]
                rows[h] = acc
    return out

NT = (((1,), (1,)), ((), ()))

def halves(value):
    high = value.astype(jnp.bfloat16)
    return high, (value - high.astype(jnp.float32)).astype(jnp.bfloat16)

def mul2(lh, ll, rh, rl):
    both = jnp.concatenate([lh, ll], axis=1)
    twice = jnp.concatenate([rh, rh], axis=1)
    first = lax.dot_general(both, twice, NT, preferred_element_type=jnp.float32)
    return first + lax.dot_general(lh, rl, NT, preferred_element_type=jnp.float32)


def mul3(lh, ll, rh, rl):
    def one(x, y):
        return lax.dot_general(x, y, NT, preferred_element_type=jnp.float32)
    return one(lh, rh) + (one(lh, rl) + one(ll, rh))

MESH = pl.DeviceIdType.MESH


def lead_place(i, k, count):
    first = early_count(count)
    if k < first:
        return 0, i, k
    apart, ring = i - k, count - first
    source, slot = (i, apart) if 2 * apart <= ring else (k, ring - apart)
    return 1, source, slot


def early_count(count):
    return max(2, count // 4)


def update_kernel(
    rank_ref, left_ref, right_ref, tiles_ref, y_ref,
    vu_all, vv_all, x_ref, part_ref,
    vu_ref, diag_ref, lead_a, lead_b, blocks_a, blocks_b, piece_a, piece_b, pairs, um, own_mu, high, low, work, wh, wl,
    uv_send, uv_recv, fw_send, fw_recv, cut_send, cut_recv, ring_send, ring_recv,
    flat_send, flat_recv, pair_send, pair_recv, vcut_send, vcut_recv, vflat_send, vflat_recv, local_sem,
):
    rows, cols = cut_send.shape[1], vu_all.shape[1]
    side = {4: 2, 16: 4}[rows]
    depth = cols // 2
    early = early_count(cols)
    late = cols - early
    thin = piece_a.shape[1]
    p, c = lax.axis_index("row"), lax.axis_index("col")
    z, core = c // 2, lax.rem(c, 2)
    sibling = c + 1 - 2 * core

    order = y_ref.shape[1]
    count = cols
    total = order + y_ref.shape[0]

    def along(d):
        return (p, 2 * lax.rem(z + d, depth) + core)

    def shift(q, axis, steps):
        x, y = q // side, lax.rem(q, side)
        if axis == 0:
            return lax.rem(x + steps + side, side) * side + y
        return x * side + lax.rem(y + steps + side, side)

    def remote(src, dst, send, recv, where):
        return pltpu.make_async_remote_copy(
            src_ref=src, dst_ref=dst, send_sem=send, recv_sem=recv, device_id=where, device_id_type=MESH
        )

    def start_all(copies):
        for copy in copies:
            copy.start()

    fetch = pltpu.make_async_copy(tiles_ref.at[0, 0], diag_ref, local_sem.at[2])

    @pl.when(p == 0)
    def _():
        fetch.start()

    barrier = pltpu.get_barrier_semaphore()
    partners = [along(d) for d in range(1, depth)] + [(p, sibling)] + [(lax.rem(p + d, rows), c) for d in range(1, rows)]
    for where in partners:
        pl.semaphore_signal(barrier, inc=1, device_id=where, device_id_type=MESH)
    for a in range(2):
        wide_lanes = lax.broadcasted_iota(jnp.int32, (BLK, BLK), 1)
        joined = jnp.concatenate([right_ref[a, 0], left_ref[a, 0]], axis=1).astype(jnp.float32)
        rank = rank_ref[a, 0]
        live = lax.rem(wide_lanes, BLK // 2) < rank
        vu_ref[a] = jnp.where(live, joined, 0.0).astype(jnp.bfloat16)
    pl.semaphore_wait(barrier, len(partners))

    spreads = []
    for a in range(2):
        first = [
            remote(vu_ref.at[a], vu_all.at[a, c], uv_send.at[a, d], uv_recv.at[a, d], along(d)) for d in range(1, depth)
        ]
        held = [vu_all.at[a, 2 * lax.rem(z + depth - d, depth) + core] for d in range(depth)]
        later = [remote(vu_ref.at[a], vu_all.at[a, c], fw_send.at[a, 0], fw_recv.at[a, 0], (p, sibling))] + [
            remote(held[d], held[d], fw_send.at[a, d], fw_recv.at[a, d], (p, sibling)) for d in range(1, depth)
        ]
        spreads.append((first, later))

    def spread_start(a):
        first, later = spreads[a]
        start_all(first)
        later[0].start()
        vu_all[a, c] = vu_ref[a]

    def spread_pass(a):
        first, later = spreads[a]
        for one, two in zip(first, later[1:]):
            one.wait_recv()
            two.start()

    def spread_end(a):
        for copy in spreads[a][1]:
            copy.wait_recv()

    phases = []
    for f, (blocks, piece) in enumerate(((blocks_a, piece_a), (blocks_b, piece_b))):
        wide = blocks.shape[0]
        mine = piece.at[pl.ds(z * wide, wide)]
        cuts = [
            remote(blocks.at[:, pl.ds(d * thin, thin), :], mine, cut_send.at[f, d], cut_recv.at[f], (d, c))
            for d in range(1, rows)
        ]
        ring = [remote(mine, mine, ring_send.at[f, d], ring_recv.at[f, d], along(d)) for d in range(1, depth)]
        phases.append((cuts, ring, mine))

    def plane_gather(region, origin, send, recv, shared):
        hops, shares = {}, {}
        units = {}

        def add(k, slot, src, dst, axis, steps):
            hops[k, slot] = remote(src, dst, send.at[k, slot], recv.at[k, slot], (shift(p, axis, steps), c))

        def share(k, index, q, src=None):
            if shared is not None:
                held = region(q, k, None)
                shares[k, index] = remote(
                    held if src is None else src, held, shared[0].at[k, index], shared[1].at[k, index], (p, sibling)
                )

        for k in range(2):
            one, two = 1 - k, k
            src, whole = origin(k), region(p, k, None)
            add(k, 0, src, whole, one, 1)
            if side == 4:
                add(k, 1, src, whole, one, -1)
                back, ahead = region(shift(p, one, -1), k, 0), region(shift(p, one, 1), k, 1)
                add(k, 2, back, back, one, 1)
                add(k, 3, ahead, ahead, one, -1)
            steps = (0, -1, 1, 2)[:side]
            for t, step in enumerate(steps):
                q = shift(p, one, step) if step else p
                whole = region(q, k, None)
                src = origin(k) if t == 0 else whole
                add(k, 4 + 4 * t, src, whole, two, 1)
                share(k, 4 * t, q, src)
                share(k, 4 * t + 1, shift(q, two, -1))
                if side == 4:
                    add(k, 5 + 4 * t, src, whole, two, -1)
                    back, ahead = region(shift(q, two, -1), k, 0), region(shift(q, two, 1), k, 1)
                    add(k, 6 + 4 * t, back, back, two, 1)
                    add(k, 7 + 4 * t, ahead, ahead, two, -1)
                    share(k, 4 * t + 2, shift(q, two, 1))
                    share(k, 4 * t + 3, shift(q, two, 2))

        def go(k, slot):
            if (k, slot) in hops:
                hops[k, slot].start()

        def arrived(k, slot):
            if (k, slot) in hops:
                hops[k, slot].wait_recv()

        def hand(k, index):
            if (k, index) in shares:
                shares[k, index].start()

        def fan(k, t):
            go(k, 4 + 4 * t)
            go(k, 5 + 4 * t)
            hand(k, 4 * t)

        def relay(t):
            for k in range(2):
                arrived(k, 4 + 4 * t)
                go(k, 6 + 4 * t)
                hand(k, 4 * t + 1)
                arrived(k, 5 + 4 * t)
                go(k, 7 + 4 * t)
                hand(k, 4 * t + 2)

        def stage(number):
            if number == 0:
                for k in range(2):
                    go(k, 0)
                    go(k, 1)
                    fan(k, 0)
            if number == 1:
                for k in range(2):
                    arrived(k, 0)
                    go(k, 2)
                    fan(k, 1)
                if side == 4:
                    for k in range(2):
                        arrived(k, 1)
                        go(k, 3)
                        fan(k, 2)
            if number == 2:
                relay(0)
                if side == 4:
                    for k in range(2):
                        arrived(k, 2)
                        arrived(k, 3)
                        fan(k, 3)
            if number == 3:
                for t in range(1, side):
                    relay(t)
            if number == 4 and side == 4:
                for t in range(side):
                    for k in range(2):
                        arrived(k, 6 + 4 * t)
                        arrived(k, 7 + 4 * t)
                        hand(k, 4 * t + 3)
            if number == 5:
                for copy in shares.values():
                    copy.wait_recv()
            if number == 6:
                for copy in list(hops.values()) + list(shares.values()):
                    copy.wait_send()

        return stage

    def lead_stages(f, lead, piece, skip):
        slots = lead.shape[1]
        middle, quarter = slots // 2, slots // 4
        edges = [(0, quarter, middle), (middle, middle + quarter, slots)]

        def region(q, k, part):
            lo, mid, hi = edges[k]
            lo, hi = {None: (lo, hi), 0: (lo, mid), 1: (mid, hi)}[part]
            return lead.at[core, pl.ds(lo, hi - lo), pl.ds(pl.multiple_of(q * thin, thin), thin), :]

        def origin(k):
            lo, mid, hi = edges[k]
            return piece.at[pl.ds(skip + lo, hi - lo)]

        stage = plane_gather(region, origin, flat_send.at[f], flat_recv.at[f], (pair_send.at[f], pair_recv.at[f]))
        keep = pltpu.make_async_copy(
            piece.at[pl.ds(skip, slots)],
            lead.at[core, :, pl.ds(pl.multiple_of(p * thin, thin), thin), :],
            local_sem.at[f],
        )
        return stage, keep

    skip_b = (early // 2) * blocks_b.shape[0]
    stage_a, keep_a = lead_stages(0, lead_a, piece_a, 0)
    stage_b, keep_b = lead_stages(1, lead_b, piece_b, skip_b)

    def pair_region(q, k, part):
        half = BLK // 2
        lo, size = {None: (0, half), 0: (0, half // 2), 1: (half // 2, half // 2)}[part]
        return vv_all.at[q, pl.ds(k * half + lo, size)]

    stage_v = plane_gather(pair_region, lambda k: pair_region(p, k, None), vflat_send, vflat_recv, None)
    vcuts = [
        remote(pairs.at[d], vv_all.at[lax.rem(p + d, rows)], vcut_send.at[d], vcut_recv, (lax.rem(p + d, rows), c))
        for d in range(1, rows)
    ]
    turns = [lax.rem(s + rows - p, rows) for s in range(cols)]

    def lead_block(other):
        fix = lax.dot_general(own_mu[...], um[other], NT, preferred_element_type=jnp.float32)
        return diag_ref[:, pl.ds(pl.multiple_of(other * BLK, BLK), BLK)] - 0.5 * fix

    spread_start(0)
    spread_pass(0)
    spread_end(0)

    @pl.when(p == 0)
    def _():
        size = BLK
        r = lax.broadcasted_iota(jnp.int32, (size, size), 0)
        l = lax.broadcasted_iota(jnp.int32, (size, size), 1)
        half = size // 2

        def dots(x, y, dims):
            return lax.dot_general(x, y, (dims, ((), ())), preferred_element_type=jnp.float32)

        flat = vu_all[0].reshape(order, size)
        gram = dots(flat, flat, ((0,), (0,)))
        core_w = jnp.where((r < half) & (l < half), gram, 0.0).astype(jnp.bfloat16)
        down = jnp.where(r == l + half, 1.0, 0.0).astype(jnp.bfloat16)
        right = jnp.where(l == r + half, 1.0, 0.0).astype(jnp.bfloat16)
        same = jnp.where((r == l) & (r >= half), 1.0, 0.0)
        low_w = dots(down, core_w, ((1,), (0,)))
        low_w16 = low_w.astype(jnp.bfloat16)
        take_mu = (low_w + same).astype(jnp.bfloat16)
        take_um = (dots(low_w16, right, ((1,), (0,))) + down.astype(jnp.float32)).astype(jnp.bfloat16)
        um[...] = dots(flat, take_um, ((1,), (0,))).astype(jnp.bfloat16).reshape(um.shape)
        fetch.wait()
        own_mu[...] = dots(vu_ref[0], take_mu, ((1,), (0,))).astype(jnp.bfloat16)
        for j in range(early):
            blocks_a[j] = lead_block(j)
        phases[0][2][...] = blocks_a[:, :thin, :]
        start_all(phases[0][0])

    @pl.when(p > 0)
    def _():
        phases[0][0][0].wait_recv()

    start_all(phases[0][1])

    @pl.when(p == 0)
    def _():
        for j in range(late // 2 + 1):
            other = early + lax.rem(c - early - j + 2 * late, late)
            block = lead_block(other)

            @pl.when(c >= other)
            def _(block=block, j=j):
                blocks_b[j] = block

            @pl.when(c < other)
            def _(block=block, j=j):
                blocks_b[j] = block.T
        phases[1][2][...] = blocks_b[:, :thin, :]
        start_all(phases[1][0])

    for copy in phases[0][1]:
        copy.wait_recv()
    keep_a.start()
    stage_a(0)

    @pl.when(p > 0)
    def _():
        phases[1][0][0].wait_recv()

    stage_a(1)
    start_all(phases[1][1])
    stage_a(2)
    stage_a(3)
    stage_a(4)
    for copy in phases[1][1]:
        copy.wait_recv()
    keep_b.start()
    stage_b(0)
    spread_start(1)
    keep_a.wait()
    stage_a(5)

    def build_pairs():
        @pl.when(p == c)
        def _():
            for s in range(cols):
                lanes = lax.broadcasted_iota(jnp.int32, (BLK, BLK), 1)
                lefts = vu_all[0, s].astype(jnp.float32)
                rights = pltpu.roll(vu_all[1, s].astype(jnp.float32), BLK // 2, 1)
                pairs[turns[s]] = jnp.where(lanes < BLK // 2, lefts, rights).astype(jnp.bfloat16)
            vv_all[p] = pairs[0]
            start_all(vcuts)

    def take_pairs():
        @pl.when(p != c)
        def _():
            vcuts[0].wait_recv()

    def errands(s):
        if s < early:
            stage_b(s + 1)
        if s == early - 1:
            for number in range(early + 1, 6):
                stage_b(number)
            keep_b.wait()
        if count == 16:
            plan = {4: [lambda: spread_pass(1)], 5: [lambda: spread_end(1), build_pairs], 6: [take_pairs, lambda: stage_v(0)],
                    7: [lambda: stage_v(1)], 8: [lambda: stage_v(2)], 9: [lambda: stage_v(3)], 10: [lambda: stage_v(4)]}
        else:
            plan = {3: [lambda: spread_pass(1), lambda: spread_end(1), build_pairs, take_pairs] + [lambda n=n: stage_v(n) for n in range(5)]}
        for act in plan.get(s, []):
            act()

    def block_of(i, k):
        if i < k:
            return jnp.zeros((BLK, BLK), jnp.float32)
        phase, source, slot = lead_place(i, k, count)
        if phase == 0:
            return lead_a[source % 2, (source // 2) * early + slot]
        return lead_b[source % 2, (source // 2 - early // 2) * (late // 2 + 1) + slot]

    def given(r0, r1, k):
        lo = k * BLK
        parts = [block_of(r // BLK, k) for r in range(r0, min(r1, order), BLK)]
        if r1 > order:
            parts.append(y_ref[max(r0, order) - order:r1 - order, lo:lo + BLK])
        return parts[0] if len(parts) == 1 else jnp.concatenate(parts, axis=0)

    def pair_given(r0, r1, k):
        return jnp.concatenate([given(r0, r1, k), given(r0, r1, k + 1)], axis=1)

    def spans(start, size):
        return [(r, min(r + size, total)) for r in range(start, total, size)]

    for r0, r1 in spans(0, 2 * BLK):
        work[r0:r1, :] = pair_given(r0, r1, 0)
    part_ref[...] = jnp.zeros_like(part_ref)

    def step(k, carry):
        base = pl.multiple_of(k * BLK, BLK)
        flank = pl.ds(pl.multiple_of(lax.rem(k, 2) * BLK, BLK), BLK)
        inverse = invert_factor([work[pl.ds(base + g * GRP, GRP), flank] for g in range(BLK // GRP)])
        high_part, low_part = halves(jnp.concatenate(inverse, axis=0))
        wh[...] = high_part
        wl[...] = low_part

        for s in range(count):
            @pl.when(k == s)
            def _(s=s):
                lo, hi = s * BLK, s * BLK + BLK
                left = (s % 2) * BLK
                errands(s)
                for r0, r1 in spans(lo, 8 * BLK):
                    sh, sl = halves(work[r0:r1, left:left + BLK])
                    panel = mul2(sh, sl, wh[...], wl[...])
                    ph, pl_ = halves(panel)
                    high[r0:r1, lo:hi] = ph
                    low[r0:r1, lo:hi] = pl_
                    work[r0:r1, left:left + BLK] = panel
                x_ref[:, lo:hi] = work[order:order + x_ref.shape[0], left:left + BLK]

                @pl.when(jnp.logical_and(c == s, p >= s))
                def _():
                    block = work[pl.ds(pl.multiple_of(p * BLK, BLK), BLK), left:left + BLK]
                    r = lax.broadcasted_iota(jnp.int32, (BLK, BLK), 0)
                    l = lax.broadcasted_iota(jnp.int32, (BLK, BLK), 1)
                    part_ref[...] = jnp.where((p > s) | (r >= l), block, 0.0)

                if s % 2 == 0 and s + 1 < count:
                    for r0, r1 in spans(hi, 8 * BLK):
                        work[r0:r1, BLK:] = work[r0:r1, BLK:] - mul2(
                            high[r0:r1, lo:hi], low[r0:r1, lo:hi],
                            high[hi:hi + BLK, lo:hi], low[hi:hi + BLK, lo:hi])
                if s % 2 == 1 and s + 1 < count:
                    end = hi + 2 * BLK
                    for r0, r1 in spans(hi, 8 * BLK):
                        work[r0:r1, :] = pair_given(r0, r1, s + 1) - mul3(
                            high[r0:r1, :hi], low[r0:r1, :hi],
                            high[hi:end, :hi], low[hi:end, :hi])
        return carry

    lax.fori_loop(0, count, step, 0)

    stage_a(6)
    stage_b(6)
    stage_v(6)
    for first, later in spreads:
        for copy in first + later:
            copy.wait_send()
    for cuts, ring, mine in phases:
        for copy in ring:
            copy.wait_send()

    @pl.when(p == 0)
    def _():
        for cuts, ring, mine in phases:
            for copy in cuts:
                copy.wait_send()

    @pl.when(p == c)
    def _():
        for copy in vcuts:
            copy.wait_send()


def update_call(rank, left, right_factor, tiles, right, narrow):
    rows, cols = lax.axis_size("row"), lax.axis_size("col")
    depth, thin = cols // 2, BLK // rows
    extra, order = right.shape
    early = early_count(cols)
    late = (cols - early) // 2 + 1
    vm = pl.BlockSpec(memory_space=pltpu.VMEM)
    dma = pltpu.SemaphoreType.DMA
    wide, half = jnp.float32, jnp.bfloat16
    return pl.pallas_call(
        update_kernel,
        out_shape=(
            jax.ShapeDtypeStruct((2, cols, BLK, BLK), half),
            jax.ShapeDtypeStruct((rows, BLK, BLK), half),
            jax.ShapeDtypeStruct((narrow, order), wide),
            jax.ShapeDtypeStruct((BLK, BLK), wide),
        ),
        in_specs=[pl.BlockSpec(memory_space=pltpu.SMEM), vm, vm, pl.BlockSpec(memory_space=pl.ANY), vm],
        out_specs=(vm, vm, vm, vm),
        scratch_shapes=[
            pltpu.VMEM((2, BLK, BLK), half),
            pltpu.VMEM((BLK, order), wide),
            pltpu.VMEM((2, depth * early, BLK, BLK), wide),
            pltpu.VMEM((2, (depth - early // 2) * late, BLK, BLK), wide),
            pltpu.VMEM((early, BLK, BLK), wide),
            pltpu.VMEM((late, BLK, BLK), wide),
            pltpu.VMEM((depth * early, thin, BLK), wide),
            pltpu.VMEM((depth * late, thin, BLK), wide),
            pltpu.VMEM((rows, BLK, BLK), half),
            pltpu.VMEM((cols, BLK, BLK), half),
            pltpu.VMEM((BLK, BLK), half),
            pltpu.VMEM((order + extra, order), half),
            pltpu.VMEM((order + extra, order), half),
            pltpu.VMEM((order + extra, 2 * BLK), wide),
            pltpu.VMEM((BLK, BLK), half),
            pltpu.VMEM((BLK, BLK), half),
            dma((2, depth)), dma((2, depth)), dma((2, depth)), dma((2, depth)),
            dma((2, rows)), dma((2,)), dma((2, depth)), dma((2, depth)),
            dma((2, 2, 20)), dma((2, 2, 20)), dma((2, 2, 16)), dma((2, 2, 16)),
            dma((rows,)), dma, dma((2, 20)), dma((2, 20)), dma((3,)),
        ],
        compiler_params=pltpu.CompilerParams(
            collective_id=0, has_side_effects=True, vmem_limit_bytes=56 * 2**20
        ),
        cost_estimate=pl.CostEstimate(flops=10**11, bytes_accessed=2 * 10**7, transcendentals=0),
    )(rank, left, right_factor, tiles, right)


def body(pan_left, pan_right, panel_rank, diag_tiles, col_right, column_rank):
    tile_rows = pan_left.shape[0]
    slab_rows = pan_left.shape[2]
    rank_width = pan_left.shape[3]
    tile_order = diag_tiles.shape[3]
    row_count = lax.axis_size("row")
    col_count = lax.axis_size("col")
    row_index = lax.axis_index("row")
    col_index = lax.axis_index("col")
    col_tiles = tile_rows * row_count // col_count
    narrow_rows = col_right.shape[2]
    rank_ids = lax.broadcasted_iota(jnp.int32, col_right.shape, 2) + col_index * narrow_rows
    tile_ids = lax.broadcasted_iota(jnp.int32, col_right.shape, 0) * row_count + row_index
    keep_right = (rank_ids < column_rank[:, :, None, None]) & (tile_ids >= 1)
    right_kept = jnp.where(keep_right, col_right, jnp.zeros_like(col_right))
    right_side = right_kept.astype(jnp.float32).reshape(-1, tile_order)
    count = right_side.shape[0]
    right_side = jnp.pad(right_side, ((0, -count % 16), (0, 0)))
    vu_all, vv_all, solved, lead_part = update_call(
        panel_rank, pan_left, pan_right, diag_tiles, right_side, count
    )
    flat_vu = vu_all.reshape(tile_rows, tile_order, 2 * rank_width)
    right_tiles, left_tiles = flat_vu[:, :, :rank_width], flat_vu[:, :, rank_width:]
    theirs = vv_all.reshape(tile_order, col_tiles, rank_width)
    own_gram = jnp.einsum(
        "anr,ans->ars", right_tiles, right_tiles, preferred_element_type=jnp.float32
    ).astype(jnp.bfloat16)
    products = jnp.einsum(
        "anr,ars->ans", left_tiles, own_gram, preferred_element_type=jnp.float32
    ).astype(jnp.bfloat16)
    product_rows = lax.dynamic_slice_in_dim(products, col_index * slab_rows, slab_rows, 1)
    correction = jnp.einsum(
        "ans,ams->anm", product_rows, left_tiles, preferred_element_type=jnp.float32
    )
    diag_new = diag_tiles - correction[:, None]
    cross_gram = jnp.einsum(
        "anr,nbs->abrs", right_tiles, theirs, preferred_element_type=jnp.float32
    ).astype(jnp.bfloat16)

    col_solved = solved.reshape(col_right.shape)

    tile_update = jnp.einsum(
        "anr,abrs->abns", left_tiles, cross_gram, preferred_element_type=jnp.float32
    )
    row_ids = lax.broadcasted_iota(jnp.int32, (tile_rows, col_tiles), 0) * row_count + row_index
    col_ids = lax.broadcasted_iota(jnp.int32, (tile_rows, col_tiles), 1) * col_count + col_index
    lower_mask = (row_ids > col_ids)[:, :, None, None]
    panel_update = jnp.where(lower_mask, tile_update, jnp.zeros_like(tile_update)).astype(
        jnp.bfloat16
    )
    panel_update = panel_update.reshape(tile_rows, 1, col_tiles, 1, tile_order, rank_width)
    return (panel_update, diag_new, lead_part, col_solved)


def solution(mesh):
    placed = (
        P(None, "row", "col", None),
        P(None, "row", "col", None),
        P(None, "row"),
        P(None, "row", "col", None),
        P(None, "row", "col", None),
        P(None, "row"),
    )
    return jax.shard_map(
        body,
        mesh=mesh,
        in_specs=placed,
        out_specs=(
            P(None, "row", None, "col", None, None),
            P(None, "row", "col", None),
            P("row", "col"),
            P(None, "row", "col", None),
        ),
        check_vma=False,
    )
```

```python
import jax, jax.numpy as jnp
from jax import lax
from jax.sharding import PartitionSpec as P
from jax.experimental import pallas as pl
from jax.experimental.pallas import tpu as pltpu

BLK = 128
GRP = 8

def recip(value):
    start = pl.reciprocal(value, approx=True)
    return start * (2.0 - value * start)

def invert_factor(rows):
    count = len(rows)
    shape = (GRP, BLK)
    lanes = lax.broadcasted_iota(jnp.int32, shape, 1)
    subs = lax.broadcasted_iota(jnp.int32, shape, 0)

    def lane(value, index):
        return jnp.broadcast_to(value[:, index : index + 1], shape)

    def line(value, index):
        return jnp.broadcast_to(value[index : index + 1, :], shape)

    kept = [jnp.where(lanes == subs + g * GRP, rows[g], 0.0) for g in range(count)]
    tall = [lax.rsqrt(jnp.broadcast_to(jnp.sum(k, axis=1, keepdims=True), shape)) for k in kept]
    total = kept[0]
    for g in range(1, count):
        total = total + kept[g]
    wide = lax.rsqrt(jnp.broadcast_to(jnp.sum(total, axis=0, keepdims=True), shape))
    rows = [rows[g] * tall[g] * wide for g in range(count)]

    out = []
    edge = [lane(rows[0], k) for k in range(GRP)]
    for g in range(count):
        base = g * GRP
        here = (lanes >= base) & (lanes < base + GRP)
        last = g + 1 == count
        tri = {(i, j): line(edge[j], i) for j in range(GRP) for i in range(j, GRP)}
        cols = {h: [lane(rows[h], base + j) for j in range(GRP)] for h in range(g + 1, count)}
        if not last:
            near = list(cols[g + 1])
            edge = [lane(rows[g + 1], base + GRP + k) for k in range(GRP)]
        pivot = jnp.where(here, jnp.where(lanes - base == subs, 1.0, 0.0), rows[g])
        lines = [line(pivot, j) for j in range(GRP)]
        weight = {}
        pairs = []
        done = jnp.zeros(shape, jnp.float32)
        for j in range(0, GRP, 2):
            a, b, c = tri[j, j], tri[j + 1, j], tri[j + 1, j + 1]
            det = a * c - b * b
            r = recip(det)
            pairs.append((a, b, c, r))
            for i in range(j + 2, GRP):
                x, y = tri[i, j], tri[i, j + 1]
                u, v = c * x - b * y, a * y - b * x
                for k in range(j + 2, i + 1):
                    tri[i, k] = tri[i, k] - r * (u * tri[k, j] + v * tri[k, j + 1])
                weight[i, j], weight[i, j + 1] = u * r, v * r
                lines[i] = lines[i] - (weight[i, j] * lines[j] + weight[i, j + 1] * lines[j + 1])
            if not last:
                u = c * near[j] - b * near[j + 1]
                v = a * near[j + 1] - b * near[j]
                for k in range(GRP):
                    edge[k] = edge[k] - r * (u * line(near[j], k) + v * line(near[j + 1], k))
                for k in range(j + 2, GRP):
                    near[k] = near[k] - r * (u * tri[k, j] + v * tri[k, j + 1])
            root = lax.rsqrt(a)
            done = jnp.where(subs == j, lines[j] * root, done)
            second = (lines[j + 1] - (b * root * root) * lines[j]) * (a * root * lax.rsqrt(det))
            done = jnp.where(subs == j + 1, second, done)
        out.append(jnp.where(lanes <= subs + base, done, 0.0) * wide)
        if not last:
            back = [None] * GRP
            for j in range(GRP - 2, -1, -2):
                a, b, c, r = pairs[j // 2]
                first = r * (c * lines[j] - b * lines[j + 1])
                second = r * (a * lines[j + 1] - b * lines[j])
                for i in range(GRP - 1, j + 1, -1):
                    first = first - weight[i, j] * back[i]
                    second = second - weight[i, j + 1] * back[i]
                back[j], back[j + 1] = first, second
            for h in range(g + 1, count):
                acc = jnp.where(here, 0.0, rows[h])
                for j in range(GRP - 1, -1, -1):
                    acc = acc - cols[h][j] * back[j]
                rows[h] = acc
    return out

NT = (((1,), (1,)), ((), ()))

def halves(value):
    high = value.astype(jnp.bfloat16)
    return high, (value - high.astype(jnp.float32)).astype(jnp.bfloat16)

def mul2(lh, ll, rh, rl):
    both = jnp.concatenate([lh, ll], axis=1)
    twice = jnp.concatenate([rh, rh], axis=1)
    first = lax.dot_general(both, twice, NT, preferred_element_type=jnp.float32)
    return first + lax.dot_general(lh, rl, NT, preferred_element_type=jnp.float32)


def mul3(lh, ll, rh, rl):
    def one(x, y):
        return lax.dot_general(x, y, NT, preferred_element_type=jnp.float32)
    return one(lh, rh) + (one(lh, rl) + one(ll, rh))

MESH = pl.DeviceIdType.MESH


def lead_place(i, k, count):
    first = early_count(count)
    if k < first:
        return 0, i, k
    apart, ring = i - k, count - first
    source, slot = (i, apart) if 2 * apart <= ring else (k, ring - apart)
    return 1, source, slot


def early_count(count):
    return max(2, count // 4)


def update_kernel(
    rank_ref, left_ref, right_ref, tiles_ref, y_ref,
    vu_all, vv_all, x_ref, part_ref,
    vu_ref, diag_ref, lead_a, lead_b, blocks_a, blocks_b, piece_a, piece_b, pairs, slabs, um, mu, high, low, work, wh, wl,
    uv_send, uv_recv, fw_send, fw_recv, cut_send, cut_recv, ring_send, ring_recv,
    flat_send, flat_recv, pair_send, pair_recv, vcut_send, vcut_recv, vflat_send, vflat_recv, local_sem,
):
    rows, cols = cut_send.shape[1], vu_all.shape[1]
    side = {4: 2, 16: 4}[rows]
    depth = cols // 2
    early = early_count(cols)
    late = cols - early
    thin = piece_a.shape[1]
    p, c = lax.axis_index("row"), lax.axis_index("col")
    z, core = c // 2, lax.rem(c, 2)
    sibling = c + 1 - 2 * core

    order = y_ref.shape[1]
    count = cols
    total = order + y_ref.shape[0]

    def along(d):
        return (p, 2 * lax.rem(z + d, depth) + core)

    def shift(q, axis, steps):
        x, y = q // side, lax.rem(q, side)
        if axis == 0:
            return lax.rem(x + steps + side, side) * side + y
        return x * side + lax.rem(y + steps + side, side)

    def remote(src, dst, send, recv, where):
        return pltpu.make_async_remote_copy(
            src_ref=src, dst_ref=dst, send_sem=send, recv_sem=recv, device_id=where, device_id_type=MESH
        )

    def start_all(copies):
        for copy in copies:
            copy.start()

    fetch = pltpu.make_async_copy(tiles_ref.at[0, 0], diag_ref, local_sem.at[2])

    @pl.when(p == 0)
    def _():
        fetch.start()

    barrier = pltpu.get_barrier_semaphore()
    partners = [along(d) for d in range(1, depth)] + [(p, sibling)] + [(lax.rem(p + d, rows), c) for d in range(1, rows)]
    for where in partners:
        pl.semaphore_signal(barrier, inc=1, device_id=where, device_id_type=MESH)
    for a in range(2):
        wide_lanes = lax.broadcasted_iota(jnp.int32, (BLK, BLK), 1)
        joined = jnp.concatenate([right_ref[a, 0], left_ref[a, 0]], axis=1).astype(jnp.float32)
        rank = rank_ref[a, 0]
        live = lax.rem(wide_lanes, BLK // 2) < rank
        vu_ref[a] = jnp.where(live, joined, 0.0).astype(jnp.bfloat16)
    pl.semaphore_wait(barrier, len(partners))

    spreads = []
    for a in range(2):
        first = [
            remote(vu_ref.at[a], vu_all.at[a, c], uv_send.at[a, d], uv_recv.at[a, d], along(d)) for d in range(1, depth)
        ]
        held = [vu_all.at[a, 2 * lax.rem(z + depth - d, depth) + core] for d in range(depth)]
        later = [remote(vu_ref.at[a], vu_all.at[a, c], fw_send.at[a, 0], fw_recv.at[a, 0], (p, sibling))] + [
            remote(held[d], held[d], fw_send.at[a, d], fw_recv.at[a, d], (p, sibling)) for d in range(1, depth)
        ]
        spreads.append((first, later))

    def spread_start(a):
        first, later = spreads[a]
        start_all(first)
        later[0].start()
        vu_all[a, c] = vu_ref[a]

    def spread_pass(a):
        first, later = spreads[a]
        for one, two in zip(first, later[1:]):
            one.wait_recv()
            two.start()

    def spread_end(a):
        for copy in spreads[a][1]:
            copy.wait_recv()

    phases = []
    for f, (blocks, piece) in enumerate(((blocks_a, piece_a), (blocks_b, piece_b))):
        wide = blocks.shape[0]
        mine = piece.at[pl.ds(z * wide, wide)]
        cuts = [
            remote(blocks.at[:, pl.ds(d * thin, thin), :], mine, cut_send.at[f, d], cut_recv.at[f], (d, c))
            for d in range(1, rows)
        ]
        ring = [remote(mine, mine, ring_send.at[f, d], ring_recv.at[f, d], along(d)) for d in range(1, depth)]
        phases.append((cuts, ring, mine))

    def plane_gather(region, origin, send, recv, shared):
        hops, shares = {}, {}
        units = {}

        def add(k, slot, src, dst, axis, steps):
            hops[k, slot] = remote(src, dst, send.at[k, slot], recv.at[k, slot], (shift(p, axis, steps), c))

        def share(k, index, q, src=None):
            if shared is not None:
                held = region(q, k, None)
                shares[k, index] = remote(
                    held if src is None else src, held, shared[0].at[k, index], shared[1].at[k, index], (p, sibling)
                )

        for k in range(2):
            one, two = 1 - k, k
            src, whole = origin(k), region(p, k, None)
            add(k, 0, src, whole, one, 1)
            if side == 4:
                add(k, 1, src, whole, one, -1)
                back, ahead = region(shift(p, one, -1), k, 0), region(shift(p, one, 1), k, 1)
                add(k, 2, back, back, one, 1)
                add(k, 3, ahead, ahead, one, -1)
            steps = (0, -1, 1, 2)[:side]
            for t, step in enumerate(steps):
                q = shift(p, one, step) if step else p
                whole = region(q, k, None)
                src = origin(k) if t == 0 else whole
                add(k, 4 + 4 * t, src, whole, two, 1)
                share(k, 4 * t, q, src)
                share(k, 4 * t + 1, shift(q, two, -1))
                if side == 4:
                    add(k, 5 + 4 * t, src, whole, two, -1)
                    back, ahead = region(shift(q, two, -1), k, 0), region(shift(q, two, 1), k, 1)
                    add(k, 6 + 4 * t, back, back, two, 1)
                    add(k, 7 + 4 * t, ahead, ahead, two, -1)
                    share(k, 4 * t + 2, shift(q, two, 1))
                    share(k, 4 * t + 3, shift(q, two, 2))

        def go(k, slot):
            if (k, slot) in hops:
                hops[k, slot].start()

        def arrived(k, slot):
            if (k, slot) in hops:
                hops[k, slot].wait_recv()

        def hand(k, index):
            if (k, index) in shares:
                shares[k, index].start()

        def fan(k, t):
            go(k, 4 + 4 * t)
            go(k, 5 + 4 * t)
            hand(k, 4 * t)

        def relay(t):
            for k in range(2):
                arrived(k, 4 + 4 * t)
                go(k, 6 + 4 * t)
                hand(k, 4 * t + 1)
                arrived(k, 5 + 4 * t)
                go(k, 7 + 4 * t)
                hand(k, 4 * t + 2)

        def stage(number):
            if number == 0:
                for k in range(2):
                    go(k, 0)
                    go(k, 1)
                    fan(k, 0)
            if number == 1:
                for k in range(2):
                    arrived(k, 0)
                    go(k, 2)
                    fan(k, 1)
                if side == 4:
                    for k in range(2):
                        arrived(k, 1)
                        go(k, 3)
                        fan(k, 2)
            if number == 2:
                relay(0)
                if side == 4:
                    for k in range(2):
                        arrived(k, 2)
                        arrived(k, 3)
                        fan(k, 3)
            if number == 3:
                for t in range(1, side):
                    relay(t)
            if number == 4 and side == 4:
                for t in range(side):
                    for k in range(2):
                        arrived(k, 6 + 4 * t)
                        arrived(k, 7 + 4 * t)
                        hand(k, 4 * t + 3)
            if number == 5:
                for copy in shares.values():
                    copy.wait_recv()
            if number == 6:
                for copy in list(hops.values()) + list(shares.values()):
                    copy.wait_send()

        return stage

    def lead_stages(f, lead, piece, skip):
        slots = lead.shape[1]
        middle, quarter = slots // 2, slots // 4
        edges = [(0, quarter, middle), (middle, middle + quarter, slots)]

        def region(q, k, part):
            lo, mid, hi = edges[k]
            lo, hi = {None: (lo, hi), 0: (lo, mid), 1: (mid, hi)}[part]
            return lead.at[core, pl.ds(lo, hi - lo), pl.ds(pl.multiple_of(q * thin, thin), thin), :]

        def origin(k):
            lo, mid, hi = edges[k]
            return piece.at[pl.ds(skip + lo, hi - lo)]

        stage = plane_gather(region, origin, flat_send.at[f], flat_recv.at[f], (pair_send.at[f], pair_recv.at[f]))
        keep = pltpu.make_async_copy(
            piece.at[pl.ds(skip, slots)],
            lead.at[core, :, pl.ds(pl.multiple_of(p * thin, thin), thin), :],
            local_sem.at[f],
        )
        return stage, keep

    skip_b = (early // 2) * blocks_b.shape[0]
    stage_a, keep_a = lead_stages(0, lead_a, piece_a, 0)
    stage_b, keep_b = lead_stages(1, lead_b, piece_b, skip_b)

    def pair_region(q, k, part):
        half = BLK // 2
        lo, size = {None: (0, half), 0: (0, half // 2), 1: (half // 2, half // 2)}[part]
        return vv_all.at[q, pl.ds(k * half + lo, size)]

    stage_v = plane_gather(pair_region, lambda k: pair_region(p, k, None), vflat_send, vflat_recv, None)
    vcuts = [
        remote(pairs.at[d], vv_all.at[lax.rem(p + d, rows)], vcut_send.at[d], vcut_recv, (lax.rem(p + d, rows), c))
        for d in range(1, rows)
    ]
    turns = [lax.rem(s + rows - p, rows) for s in range(cols)]

    @pl.when(p == 0)
    def _():
        fetch.wait()
        for j in range(early):
            blocks_a[j] = diag_ref[:, j * BLK:(j + 1) * BLK]
        blocks_a[early] = vu_ref[0].astype(jnp.float32)
        phases[0][2][...] = blocks_a[:, :thin, :]
        start_all(phases[0][0])

    @pl.when(p > 0)
    def _():
        phases[0][0][0].wait_recv()

    start_all(phases[0][1])

    @pl.when(p == 0)
    def _():
        for j in range(late // 2 + 1):
            other = early + lax.rem(c - early - j + 2 * late, late)
            block = diag_ref[:, pl.ds(pl.multiple_of(other * BLK, BLK), BLK)]

            @pl.when(c >= other)
            def _(block=block, j=j):
                blocks_b[j] = block

            @pl.when(c < other)
            def _(block=block, j=j):
                blocks_b[j] = block.T
        phases[1][2][...] = blocks_b[:, :thin, :]
        start_all(phases[1][0])

    for copy in phases[0][1]:
        copy.wait_recv()
    keep_a.start()
    stage_a(0)

    @pl.when(p > 0)
    def _():
        phases[1][0][0].wait_recv()

    stage_a(1)
    start_all(phases[1][1])
    stage_a(2)
    stage_a(3)
    stage_a(4)
    for copy in phases[1][1]:
        copy.wait_recv()
    keep_b.start()
    stage_b(0)
    spread_start(0)
    spread_start(1)
    keep_a.wait()
    stage_a(5)

    r = lax.broadcasted_iota(jnp.int32, (BLK, BLK), 0)
    l = lax.broadcasted_iota(jnp.int32, (BLK, BLK), 1)
    half = BLK // 2

    def dots(x, y, dims):
        return lax.dot_general(x, y, (dims, ((), ())), preferred_element_type=jnp.float32)

    for s in range(cols):
        slabs[s * BLK:(s + 1) * BLK, :] = lead_a[s % 2, (s // 2) * (early + 1) + early].astype(jnp.bfloat16)
    gram = dots(slabs[...], slabs[...], ((0,), (0,)))
    core_w = jnp.where((r < half) & (l < half), gram, 0.0).astype(jnp.bfloat16)
    down = jnp.where(r == l + half, 1.0, 0.0).astype(jnp.bfloat16)
    right = jnp.where(l == r + half, 1.0, 0.0).astype(jnp.bfloat16)
    same = jnp.where((r == l) & (r >= half), 1.0, 0.0)
    low_w = dots(down, core_w, ((1,), (0,)))
    take_mu = (low_w + same).astype(jnp.bfloat16)
    take_um = (dots(low_w.astype(jnp.bfloat16), right, ((1,), (0,))) + down.astype(jnp.float32)).astype(jnp.bfloat16)
    um[...] = dots(slabs[...], take_um, ((1,), (0,))).astype(jnp.bfloat16)
    mu[:order, :] = (0.5 * dots(slabs[...], take_mu, ((1,), (0,)))).astype(jnp.bfloat16)
    mu[order:, :] = jnp.zeros((total - order, BLK), jnp.bfloat16)

    def build_pairs():
        @pl.when(p == c)
        def _():
            for s in range(cols):
                lanes = lax.broadcasted_iota(jnp.int32, (BLK, BLK), 1)
                lefts = vu_all[0, s].astype(jnp.float32)
                rights = pltpu.roll(vu_all[1, s].astype(jnp.float32), BLK // 2, 1)
                pairs[turns[s]] = jnp.where(lanes < BLK // 2, lefts, rights).astype(jnp.bfloat16)
            vv_all[p] = pairs[0]
            start_all(vcuts)

    def take_pairs():
        @pl.when(p != c)
        def _():
            vcuts[0].wait_recv()

    def errands(s):
        if s < early:
            stage_b(s + 1)
        if s == early - 1:
            for number in range(early + 1, 6):
                stage_b(number)
            keep_b.wait()
        if count == 16:
            plan = {4: [lambda: spread_pass(0), lambda: spread_pass(1)], 5: [lambda: spread_end(0), lambda: spread_end(1), build_pairs], 6: [take_pairs, lambda: stage_v(0)],
                    7: [lambda: stage_v(1)], 8: [lambda: stage_v(2)], 9: [lambda: stage_v(3)], 10: [lambda: stage_v(4)]}
        else:
            plan = {3: [lambda: spread_pass(0), lambda: spread_end(0), lambda: spread_pass(1), lambda: spread_end(1), build_pairs, take_pairs] + [lambda n=n: stage_v(n) for n in range(5)]}
        for act in plan.get(s, []):
            act()

    def block_of(i, k):
        if i < k:
            return jnp.zeros((BLK, BLK), jnp.float32)
        phase, source, slot = lead_place(i, k, count)
        if phase == 0:
            return lead_a[source % 2, (source // 2) * (early + 1) + slot]
        return lead_b[source % 2, (source // 2 - early // 2) * (late // 2 + 1) + slot]

    def given(r0, r1, k):
        lo = k * BLK
        parts = [block_of(r // BLK, k) for r in range(r0, min(r1, order), BLK)]
        if r1 > order:
            parts.append(y_ref[max(r0, order) - order:r1 - order, lo:lo + BLK])
        return parts[0] if len(parts) == 1 else jnp.concatenate(parts, axis=0)

    def pair_given(r0, r1, k):
        raw = jnp.concatenate([given(r0, r1, k), given(r0, r1, k + 1)], axis=1)
        return raw - dots(mu[r0:r1, :], um[k * BLK:(k + 2) * BLK, :], ((1,), (1,)))

    def spans(start, size):
        return [(r, min(r + size, total)) for r in range(start, total, size)]

    for r0, r1 in spans(0, 2 * BLK):
        work[r0:r1, :] = pair_given(r0, r1, 0)
    part_ref[...] = jnp.zeros_like(part_ref)

    def step(k, carry):
        base = pl.multiple_of(k * BLK, BLK)
        flank = pl.ds(pl.multiple_of(lax.rem(k, 2) * BLK, BLK), BLK)
        inverse = invert_factor([work[pl.ds(base + g * GRP, GRP), flank] for g in range(BLK // GRP)])
        high_part, low_part = halves(jnp.concatenate(inverse, axis=0))
        wh[...] = high_part
        wl[...] = low_part

        for s in range(count):
            @pl.when(k == s)
            def _(s=s):
                lo, hi = s * BLK, s * BLK + BLK
                left = (s % 2) * BLK
                errands(s)
                for r0, r1 in spans(lo, 8 * BLK):
                    sh, sl = halves(work[r0:r1, left:left + BLK])
                    panel = mul2(sh, sl, wh[...], wl[...])
                    ph, pl_ = halves(panel)
                    high[r0:r1, lo:hi] = ph
                    low[r0:r1, lo:hi] = pl_
                    work[r0:r1, left:left + BLK] = panel
                x_ref[:, lo:hi] = work[order:order + x_ref.shape[0], left:left + BLK]

                @pl.when(jnp.logical_and(c == s, p >= s))
                def _():
                    block = work[pl.ds(pl.multiple_of(p * BLK, BLK), BLK), left:left + BLK]
                    r = lax.broadcasted_iota(jnp.int32, (BLK, BLK), 0)
                    l = lax.broadcasted_iota(jnp.int32, (BLK, BLK), 1)
                    part_ref[...] = jnp.where((p > s) | (r >= l), block, 0.0)

                if s % 2 == 0 and s + 1 < count:
                    for r0, r1 in spans(hi, 8 * BLK):
                        work[r0:r1, BLK:] = work[r0:r1, BLK:] - mul2(
                            high[r0:r1, lo:hi], low[r0:r1, lo:hi],
                            high[hi:hi + BLK, lo:hi], low[hi:hi + BLK, lo:hi])
                if s % 2 == 1 and s + 1 < count:
                    end = hi + 2 * BLK
                    for r0, r1 in spans(hi, 8 * BLK):
                        work[r0:r1, :] = pair_given(r0, r1, s + 1) - mul3(
                            high[r0:r1, :hi], low[r0:r1, :hi],
                            high[hi:end, :hi], low[hi:end, :hi])
        return carry

    lax.fori_loop(0, count, step, 0)

    stage_a(6)
    stage_b(6)
    stage_v(6)
    for first, later in spreads:
        for copy in first + later:
            copy.wait_send()
    for cuts, ring, mine in phases:
        for copy in ring:
            copy.wait_send()

    @pl.when(p == 0)
    def _():
        for cuts, ring, mine in phases:
            for copy in cuts:
                copy.wait_send()

    @pl.when(p == c)
    def _():
        for copy in vcuts:
            copy.wait_send()


def update_call(rank, left, right_factor, tiles, right, narrow):
    rows, cols = lax.axis_size("row"), lax.axis_size("col")
    depth, thin = cols // 2, BLK // rows
    extra, order = right.shape
    early = early_count(cols)
    late = (cols - early) // 2 + 1
    vm = pl.BlockSpec(memory_space=pltpu.VMEM)
    dma = pltpu.SemaphoreType.DMA
    wide, half = jnp.float32, jnp.bfloat16
    return pl.pallas_call(
        update_kernel,
        out_shape=(
            jax.ShapeDtypeStruct((2, cols, BLK, BLK), half),
            jax.ShapeDtypeStruct((rows, BLK, BLK), half),
            jax.ShapeDtypeStruct((narrow, order), wide),
            jax.ShapeDtypeStruct((BLK, BLK), wide),
        ),
        in_specs=[pl.BlockSpec(memory_space=pltpu.SMEM), vm, vm, pl.BlockSpec(memory_space=pl.ANY), vm],
        out_specs=(vm, vm, vm, vm),
        scratch_shapes=[
            pltpu.VMEM((2, BLK, BLK), half),
            pltpu.VMEM((BLK, order), wide),
            pltpu.VMEM((2, depth * (early + 1), BLK, BLK), wide),
            pltpu.VMEM((2, (depth - early // 2) * late, BLK, BLK), wide),
            pltpu.VMEM((early + 1, BLK, BLK), wide),
            pltpu.VMEM((late, BLK, BLK), wide),
            pltpu.VMEM((depth * (early + 1), thin, BLK), wide),
            pltpu.VMEM((depth * late, thin, BLK), wide),
            pltpu.VMEM((rows, BLK, BLK), half),
            pltpu.VMEM((order, BLK), half),
            pltpu.VMEM((order, BLK), half),
            pltpu.VMEM((order + extra, BLK), half),
            pltpu.VMEM((order + extra, order), half),
            pltpu.VMEM((order + extra, order), half),
            pltpu.VMEM((order + extra, 2 * BLK), wide),
            pltpu.VMEM((BLK, BLK), half),
            pltpu.VMEM((BLK, BLK), half),
            dma((2, depth)), dma((2, depth)), dma((2, depth)), dma((2, depth)),
            dma((2, rows)), dma((2,)), dma((2, depth)), dma((2, depth)),
            dma((2, 2, 20)), dma((2, 2, 20)), dma((2, 2, 16)), dma((2, 2, 16)),
            dma((rows,)), dma, dma((2, 20)), dma((2, 20)), dma((3,)),
        ],
        compiler_params=pltpu.CompilerParams(
            collective_id=0, has_side_effects=True, vmem_limit_bytes=56 * 2**20
        ),
        cost_estimate=pl.CostEstimate(flops=10**11, bytes_accessed=2 * 10**7, transcendentals=0),
    )(rank, left, right_factor, tiles, right)


def body(pan_left, pan_right, panel_rank, diag_tiles, col_right, column_rank):
    tile_rows = pan_left.shape[0]
    slab_rows = pan_left.shape[2]
    rank_width = pan_left.shape[3]
    tile_order = diag_tiles.shape[3]
    row_count = lax.axis_size("row")
    col_count = lax.axis_size("col")
    row_index = lax.axis_index("row")
    col_index = lax.axis_index("col")
    col_tiles = tile_rows * row_count // col_count
    narrow_rows = col_right.shape[2]
    rank_ids = lax.broadcasted_iota(jnp.int32, col_right.shape, 2) + col_index * narrow_rows
    tile_ids = lax.broadcasted_iota(jnp.int32, col_right.shape, 0) * row_count + row_index
    keep_right = (rank_ids < column_rank[:, :, None, None]) & (tile_ids >= 1)
    right_kept = jnp.where(keep_right, col_right, jnp.zeros_like(col_right))
    right_side = right_kept.astype(jnp.float32).reshape(-1, tile_order)
    count = right_side.shape[0]
    right_side = jnp.pad(right_side, ((0, -count % 16), (0, 0)))
    vu_all, vv_all, solved, lead_part = update_call(
        panel_rank, pan_left, pan_right, diag_tiles, right_side, count
    )
    flat_vu = vu_all.reshape(tile_rows, tile_order, 2 * rank_width)
    right_tiles, left_tiles = flat_vu[:, :, :rank_width], flat_vu[:, :, rank_width:]
    theirs = vv_all.reshape(tile_order, col_tiles, rank_width)
    own_gram = jnp.einsum(
        "anr,ans->ars", right_tiles, right_tiles, preferred_element_type=jnp.float32
    ).astype(jnp.bfloat16)
    products = jnp.einsum(
        "anr,ars->ans", left_tiles, own_gram, preferred_element_type=jnp.float32
    ).astype(jnp.bfloat16)
    product_rows = lax.dynamic_slice_in_dim(products, col_index * slab_rows, slab_rows, 1)
    correction = jnp.einsum(
        "ans,ams->anm", product_rows, left_tiles, preferred_element_type=jnp.float32
    )
    diag_new = diag_tiles - correction[:, None]
    cross_gram = jnp.einsum(
        "anr,nbs->abrs", right_tiles, theirs, preferred_element_type=jnp.float32
    ).astype(jnp.bfloat16)

    col_solved = solved.reshape(col_right.shape)

    tile_update = jnp.einsum(
        "anr,abrs->abns", left_tiles, cross_gram, preferred_element_type=jnp.float32
    )
    row_ids = lax.broadcasted_iota(jnp.int32, (tile_rows, col_tiles), 0) * row_count + row_index
    col_ids = lax.broadcasted_iota(jnp.int32, (tile_rows, col_tiles), 1) * col_count + col_index
    lower_mask = (row_ids > col_ids)[:, :, None, None]
    panel_update = jnp.where(lower_mask, tile_update, jnp.zeros_like(tile_update)).astype(
        jnp.bfloat16
    )
    panel_update = panel_update.reshape(tile_rows, 1, col_tiles, 1, tile_order, rank_width)
    return (panel_update, diag_new, lead_part, col_solved)


def solution(mesh):
    placed = (
        P(None, "row", "col", None),
        P(None, "row", "col", None),
        P(None, "row"),
        P(None, "row", "col", None),
        P(None, "row", "col", None),
        P(None, "row"),
    )
    return jax.shard_map(
        body,
        mesh=mesh,
        in_specs=placed,
        out_specs=(
            P(None, "row", None, "col", None, None),
            P(None, "row", "col", None),
            P("row", "col"),
            P(None, "row", "col", None),
        ),
        check_vma=False,
    )
```

```python
import jax, jax.numpy as jnp
from jax import lax
from jax.sharding import PartitionSpec as P
from jax.experimental import pallas as pl
from jax.experimental.pallas import tpu as pltpu

BLK = 128
GRP = 8

def recip(value):
    start = pl.reciprocal(value, approx=True)
    return start * (2.0 - value * start)

def invert_factor(rows):
    count = len(rows)
    shape = (GRP, BLK)
    lanes = lax.broadcasted_iota(jnp.int32, shape, 1)
    subs = lax.broadcasted_iota(jnp.int32, shape, 0)

    def lane(value, index):
        return jnp.broadcast_to(value[:, index : index + 1], shape)

    def line(value, index):
        return jnp.broadcast_to(value[index : index + 1, :], shape)

    kept = [jnp.where(lanes == subs + g * GRP, rows[g], 0.0) for g in range(count)]
    tall = [lax.rsqrt(jnp.broadcast_to(jnp.sum(k, axis=1, keepdims=True), shape)) for k in kept]
    total = kept[0]
    for g in range(1, count):
        total = total + kept[g]
    wide = lax.rsqrt(jnp.broadcast_to(jnp.sum(total, axis=0, keepdims=True), shape))
    rows = [rows[g] * tall[g] * wide for g in range(count)]

    out = []
    edge = [lane(rows[0], k) for k in range(GRP)]
    for g in range(count):
        base = g * GRP
        here = (lanes >= base) & (lanes < base + GRP)
        last = g + 1 == count
        tri = {(i, j): line(edge[j], i) for j in range(GRP) for i in range(j, GRP)}
        cols = {h: [lane(rows[h], base + j) for j in range(GRP)] for h in range(g + 1, count)}
        if not last:
            near = list(cols[g + 1])
            edge = [lane(rows[g + 1], base + GRP + k) for k in range(GRP)]
        pivot = jnp.where(here, jnp.where(lanes - base == subs, 1.0, 0.0), rows[g])
        lines = [line(pivot, j) for j in range(GRP)]
        weight = {}
        pairs = []
        done = jnp.zeros(shape, jnp.float32)
        for j in range(0, GRP, 2):
            a, b, c = tri[j, j], tri[j + 1, j], tri[j + 1, j + 1]
            det = a * c - b * b
            r = recip(det)
            pairs.append((a, b, c, r))
            for i in range(j + 2, GRP):
                x, y = tri[i, j], tri[i, j + 1]
                u, v = c * x - b * y, a * y - b * x
                for k in range(j + 2, i + 1):
                    tri[i, k] = tri[i, k] - r * (u * tri[k, j] + v * tri[k, j + 1])
                weight[i, j], weight[i, j + 1] = u * r, v * r
                lines[i] = lines[i] - (weight[i, j] * lines[j] + weight[i, j + 1] * lines[j + 1])
            if not last:
                u = c * near[j] - b * near[j + 1]
                v = a * near[j + 1] - b * near[j]
                for k in range(GRP):
                    edge[k] = edge[k] - r * (u * line(near[j], k) + v * line(near[j + 1], k))
                for k in range(j + 2, GRP):
                    near[k] = near[k] - r * (u * tri[k, j] + v * tri[k, j + 1])
            root = lax.rsqrt(a)
            done = jnp.where(subs == j, lines[j] * root, done)
            second = (lines[j + 1] - (b * root * root) * lines[j]) * (a * root * lax.rsqrt(det))
            done = jnp.where(subs == j + 1, second, done)
        out.append(jnp.where(lanes <= subs + base, done, 0.0) * wide)
        if not last:
            back = [None] * GRP
            for j in range(GRP - 2, -1, -2):
                a, b, c, r = pairs[j // 2]
                first = r * (c * lines[j] - b * lines[j + 1])
                second = r * (a * lines[j + 1] - b * lines[j])
                for i in range(GRP - 1, j + 1, -1):
                    first = first - weight[i, j] * back[i]
                    second = second - weight[i, j + 1] * back[i]
                back[j], back[j + 1] = first, second
            for h in range(g + 1, count):
                acc = jnp.where(here, 0.0, rows[h])
                for j in range(GRP - 1, -1, -1):
                    acc = acc - cols[h][j] * back[j]
                rows[h] = acc
    return out

NT = (((1,), (1,)), ((), ()))

def halves(value):
    high = value.astype(jnp.bfloat16)
    return high, (value - high.astype(jnp.float32)).astype(jnp.bfloat16)

def mul2(lh, ll, rh, rl):
    both = jnp.concatenate([lh, ll], axis=1)
    twice = jnp.concatenate([rh, rh], axis=1)
    first = lax.dot_general(both, twice, NT, preferred_element_type=jnp.float32)
    return first + lax.dot_general(lh, rl, NT, preferred_element_type=jnp.float32)


MESH = pl.DeviceIdType.MESH


def lead_place(i, k, count):
    first = early_count(count)
    if k < first:
        return 0, i, k
    apart, ring = i - k, count - first
    source, slot = (i, apart) if 2 * apart <= ring else (k, ring - apart)
    return 1, source, slot


def early_count(count):
    return max(2, count // 4)


def update_kernel(
    rank_ref, left_ref, right_ref, tiles_ref, y_ref,
    vu_all, vv_all, x_ref, part_ref,
    vu_ref, diag_ref, lead_a, lead_b, blocks_a, blocks_b, piece_a, piece_b, pairs, slabs, um, mu, high, low, work, wh, wl,
    uv_send, uv_recv, fw_send, fw_recv, cut_send, cut_recv, ring_send, ring_recv,
    flat_send, flat_recv, pair_send, pair_recv, vcut_send, vcut_recv, vflat_send, vflat_recv, local_sem,
):
    rows, cols = cut_send.shape[1], vu_all.shape[1]
    side = {4: 2, 16: 4}[rows]
    depth = cols // 2
    early = early_count(cols)
    late = cols - early
    thin = piece_a.shape[1]
    p, c = lax.axis_index("row"), lax.axis_index("col")
    z, core = c // 2, lax.rem(c, 2)
    sibling = c + 1 - 2 * core

    order = y_ref.shape[1]
    count = cols
    total = order + y_ref.shape[0]

    def along(d):
        return (p, 2 * lax.rem(z + d, depth) + core)

    def shift(q, axis, steps):
        x, y = q // side, lax.rem(q, side)
        if axis == 0:
            return lax.rem(x + steps + side, side) * side + y
        return x * side + lax.rem(y + steps + side, side)

    def remote(src, dst, send, recv, where):
        return pltpu.make_async_remote_copy(
            src_ref=src, dst_ref=dst, send_sem=send, recv_sem=recv, device_id=where, device_id_type=MESH
        )

    def start_all(copies):
        for copy in copies:
            copy.start()

    fetch = pltpu.make_async_copy(tiles_ref.at[0, 0], diag_ref, local_sem.at[2])

    @pl.when(p == 0)
    def _():
        fetch.start()

    barrier = pltpu.get_barrier_semaphore()
    partners = [along(d) for d in range(1, depth)] + [(p, sibling)] + [(lax.rem(p + d, rows), c) for d in range(1, rows)]
    for where in partners:
        pl.semaphore_signal(barrier, inc=1, device_id=where, device_id_type=MESH)
    for a in range(2):
        wide_lanes = lax.broadcasted_iota(jnp.int32, (BLK, BLK), 1)
        joined = jnp.concatenate([right_ref[a, 0], left_ref[a, 0]], axis=1).astype(jnp.float32)
        rank = rank_ref[a, 0]
        live = lax.rem(wide_lanes, BLK // 2) < rank
        vu_ref[a] = jnp.where(live, joined, 0.0).astype(jnp.bfloat16)
    pl.semaphore_wait(barrier, len(partners))

    spreads = []
    for a in range(2):
        first = [
            remote(vu_ref.at[a], vu_all.at[a, c], uv_send.at[a, d], uv_recv.at[a, d], along(d)) for d in range(1, depth)
        ]
        held = [vu_all.at[a, 2 * lax.rem(z + depth - d, depth) + core] for d in range(depth)]
        later = [remote(vu_ref.at[a], vu_all.at[a, c], fw_send.at[a, 0], fw_recv.at[a, 0], (p, sibling))] + [
            remote(held[d], held[d], fw_send.at[a, d], fw_recv.at[a, d], (p, sibling)) for d in range(1, depth)
        ]
        spreads.append((first, later))

    def spread_start(a):
        first, later = spreads[a]
        start_all(first)
        later[0].start()
        vu_all[a, c] = vu_ref[a]

    def spread_pass(a):
        first, later = spreads[a]
        for one, two in zip(first, later[1:]):
            one.wait_recv()
            two.start()

    def spread_end(a):
        for copy in spreads[a][1]:
            copy.wait_recv()

    phases = []
    for f, (blocks, piece) in enumerate(((blocks_a, piece_a), (blocks_b, piece_b))):
        wide = blocks.shape[0]
        mine = piece.at[pl.ds(z * wide, wide)]
        cuts = [
            remote(blocks.at[:, pl.ds(d * thin, thin), :], mine, cut_send.at[f, d], cut_recv.at[f], (d, c))
            for d in range(1, rows)
        ]
        ring = [remote(mine, mine, ring_send.at[f, d], ring_recv.at[f, d], along(d)) for d in range(1, depth)]
        phases.append((cuts, ring, mine))

    def plane_gather(region, origin, send, recv, shared):
        hops, shares = {}, {}
        units = {}

        def add(k, slot, src, dst, axis, steps):
            hops[k, slot] = remote(src, dst, send.at[k, slot], recv.at[k, slot], (shift(p, axis, steps), c))

        def share(k, index, q, src=None):
            if shared is not None:
                held = region(q, k, None)
                shares[k, index] = remote(
                    held if src is None else src, held, shared[0].at[k, index], shared[1].at[k, index], (p, sibling)
                )

        for k in range(2):
            one, two = 1 - k, k
            src, whole = origin(k), region(p, k, None)
            add(k, 0, src, whole, one, 1)
            if side == 4:
                add(k, 1, src, whole, one, -1)
                back, ahead = region(shift(p, one, -1), k, 0), region(shift(p, one, 1), k, 1)
                add(k, 2, back, back, one, 1)
                add(k, 3, ahead, ahead, one, -1)
            steps = (0, -1, 1, 2)[:side]
            for t, step in enumerate(steps):
                q = shift(p, one, step) if step else p
                whole = region(q, k, None)
                src = origin(k) if t == 0 else whole
                add(k, 4 + 4 * t, src, whole, two, 1)
                share(k, 4 * t, q, src)
                share(k, 4 * t + 1, shift(q, two, -1))
                if side == 4:
                    add(k, 5 + 4 * t, src, whole, two, -1)
                    back, ahead = region(shift(q, two, -1), k, 0), region(shift(q, two, 1), k, 1)
                    add(k, 6 + 4 * t, back, back, two, 1)
                    add(k, 7 + 4 * t, ahead, ahead, two, -1)
                    share(k, 4 * t + 2, shift(q, two, 1))
                    share(k, 4 * t + 3, shift(q, two, 2))

        def go(k, slot):
            if (k, slot) in hops:
                hops[k, slot].start()

        def arrived(k, slot):
            if (k, slot) in hops:
                hops[k, slot].wait_recv()

        def hand(k, index):
            if (k, index) in shares:
                shares[k, index].start()

        def fan(k, t):
            go(k, 4 + 4 * t)
            go(k, 5 + 4 * t)
            hand(k, 4 * t)

        def relay(t):
            for k in range(2):
                arrived(k, 4 + 4 * t)
                go(k, 6 + 4 * t)
                hand(k, 4 * t + 1)
                arrived(k, 5 + 4 * t)
                go(k, 7 + 4 * t)
                hand(k, 4 * t + 2)

        def stage(number):
            if number == 0:
                for k in range(2):
                    go(k, 0)
                    go(k, 1)
                    fan(k, 0)
            if number == 1:
                for k in range(2):
                    arrived(k, 0)
                    go(k, 2)
                    fan(k, 1)
                if side == 4:
                    for k in range(2):
                        arrived(k, 1)
                        go(k, 3)
                        fan(k, 2)
            if number == 2:
                relay(0)
                if side == 4:
                    for k in range(2):
                        arrived(k, 2)
                        arrived(k, 3)
                        fan(k, 3)
            if number == 3:
                for t in range(1, side):
                    relay(t)
            if number == 4 and side == 4:
                for t in range(side):
                    for k in range(2):
                        arrived(k, 6 + 4 * t)
                        arrived(k, 7 + 4 * t)
                        hand(k, 4 * t + 3)
            if number == 5:
                for copy in shares.values():
                    copy.wait_recv()
            if number == 6:
                for copy in list(hops.values()) + list(shares.values()):
                    copy.wait_send()

        return stage

    def lead_stages(f, lead, piece, skip):
        slots = lead.shape[1]
        middle, quarter = slots // 2, slots // 4
        edges = [(0, quarter, middle), (middle, middle + quarter, slots)]

        def region(q, k, part):
            lo, mid, hi = edges[k]
            lo, hi = {None: (lo, hi), 0: (lo, mid), 1: (mid, hi)}[part]
            return lead.at[core, pl.ds(lo, hi - lo), pl.ds(pl.multiple_of(q * thin, thin), thin), :]

        def origin(k):
            lo, mid, hi = edges[k]
            return piece.at[pl.ds(skip + lo, hi - lo)]

        stage = plane_gather(region, origin, flat_send.at[f], flat_recv.at[f], (pair_send.at[f], pair_recv.at[f]))
        keep = pltpu.make_async_copy(
            piece.at[pl.ds(skip, slots)],
            lead.at[core, :, pl.ds(pl.multiple_of(p * thin, thin), thin), :],
            local_sem.at[f],
        )
        return stage, keep

    skip_b = (early // 2) * blocks_b.shape[0]
    stage_a, keep_a = lead_stages(0, lead_a, piece_a, 0)
    stage_b, keep_b = lead_stages(1, lead_b, piece_b, skip_b)

    def pair_region(q, k, part):
        half = BLK // 2
        lo, size = {None: (0, half), 0: (0, half // 2), 1: (half // 2, half // 2)}[part]
        return vv_all.at[q, pl.ds(k * half + lo, size)]

    stage_v = plane_gather(pair_region, lambda k: pair_region(p, k, None), vflat_send, vflat_recv, None)
    vcuts = [
        remote(pairs.at[d], vv_all.at[lax.rem(p + d, rows)], vcut_send.at[d], vcut_recv, (lax.rem(p + d, rows), c))
        for d in range(1, rows)
    ]
    turns = [lax.rem(s + rows - p, rows) for s in range(cols)]

    @pl.when(p == 0)
    def _():
        fetch.wait()
        for j in range(early):
            blocks_a[j] = diag_ref[:, j * BLK:(j + 1) * BLK]
        blocks_a[early] = vu_ref[0].astype(jnp.float32)
        phases[0][2][...] = blocks_a[:, :thin, :]
        start_all(phases[0][0])

    @pl.when(p > 0)
    def _():
        phases[0][0][0].wait_recv()

    start_all(phases[0][1])

    @pl.when(p == 0)
    def _():
        for j in range(late // 2 + 1):
            other = early + lax.rem(c - early - j + 2 * late, late)
            block = diag_ref[:, pl.ds(pl.multiple_of(other * BLK, BLK), BLK)]

            @pl.when(c >= other)
            def _(block=block, j=j):
                blocks_b[j] = block

            @pl.when(c < other)
            def _(block=block, j=j):
                blocks_b[j] = block.T
        phases[1][2][...] = blocks_b[:, :thin, :]
        start_all(phases[1][0])

    for copy in phases[0][1]:
        copy.wait_recv()
    keep_a.start()
    stage_a(0)

    @pl.when(p > 0)
    def _():
        phases[1][0][0].wait_recv()

    stage_a(1)
    start_all(phases[1][1])
    stage_a(2)
    stage_a(3)
    stage_a(4)
    for copy in phases[1][1]:
        copy.wait_recv()
    keep_b.start()
    stage_b(0)
    spread_start(0)
    spread_start(1)
    keep_a.wait()
    stage_a(5)

    r = lax.broadcasted_iota(jnp.int32, (BLK, BLK), 0)
    l = lax.broadcasted_iota(jnp.int32, (BLK, BLK), 1)
    half = BLK // 2

    def dots(x, y, dims):
        return lax.dot_general(x, y, (dims, ((), ())), preferred_element_type=jnp.float32)

    for s in range(cols):
        slabs[s * BLK:(s + 1) * BLK, :] = lead_a[s % 2, (s // 2) * (early + 1) + early].astype(jnp.bfloat16)
    gram = dots(slabs[...], slabs[...], ((0,), (0,)))
    core_w = jnp.where((r < half) & (l < half), gram, 0.0).astype(jnp.bfloat16)
    down = jnp.where(r == l + half, 1.0, 0.0).astype(jnp.bfloat16)
    right = jnp.where(l == r + half, 1.0, 0.0).astype(jnp.bfloat16)
    same = jnp.where((r == l) & (r >= half), 1.0, 0.0)
    low_w = dots(down, core_w, ((1,), (0,)))
    take_mu = (low_w + same).astype(jnp.bfloat16)
    take_um = (dots(low_w.astype(jnp.bfloat16), right, ((1,), (0,))) + down.astype(jnp.float32)).astype(jnp.bfloat16)
    um[...] = dots(slabs[...], take_um, ((1,), (0,))).astype(jnp.bfloat16)
    mu[:order, :] = (0.5 * dots(slabs[...], take_mu, ((1,), (0,)))).astype(jnp.bfloat16)
    mu[order:, :] = jnp.zeros((total - order, BLK), jnp.bfloat16)

    def build_pairs():
        @pl.when(p == c)
        def _():
            for s in range(cols):
                lanes = lax.broadcasted_iota(jnp.int32, (BLK, BLK), 1)
                lefts = vu_all[0, s].astype(jnp.float32)
                rights = pltpu.roll(vu_all[1, s].astype(jnp.float32), BLK // 2, 1)
                pairs[turns[s]] = jnp.where(lanes < BLK // 2, lefts, rights).astype(jnp.bfloat16)
            vv_all[p] = pairs[0]
            start_all(vcuts)

    def take_pairs():
        @pl.when(p != c)
        def _():
            vcuts[0].wait_recv()

    def errands(s):
        if s < early:
            stage_b(s + 1)
        if s == early - 1:
            for number in range(early + 1, 6):
                stage_b(number)
            keep_b.wait()
        if count == 16:
            plan = {4: [lambda: spread_pass(0), lambda: spread_pass(1)], 5: [lambda: spread_end(0), lambda: spread_end(1), build_pairs], 6: [take_pairs, lambda: stage_v(0)],
                    7: [lambda: stage_v(1)], 8: [lambda: stage_v(2)], 9: [lambda: stage_v(3)], 10: [lambda: stage_v(4)]}
        else:
            plan = {3: [lambda: spread_pass(0), lambda: spread_end(0), lambda: spread_pass(1), lambda: spread_end(1), build_pairs, take_pairs] + [lambda n=n: stage_v(n) for n in range(5)]}
        for act in plan.get(s, []):
            act()

    def block_of(i, k):
        if i < k:
            return jnp.zeros((BLK, BLK), jnp.float32)
        phase, source, slot = lead_place(i, k, count)
        if phase == 0:
            return lead_a[source % 2, (source // 2) * (early + 1) + slot]
        return lead_b[source % 2, (source // 2 - early // 2) * (late // 2 + 1) + slot]

    def given(r0, r1, k):
        lo = k * BLK
        parts = [block_of(r // BLK, k) for r in range(r0, min(r1, order), BLK)]
        if r1 > order:
            parts.append(y_ref[max(r0, order) - order:r1 - order, lo:lo + BLK])
        return parts[0] if len(parts) == 1 else jnp.concatenate(parts, axis=0)

    def pair_given(r0, r1, k):
        raw = jnp.concatenate([given(r0, r1, k), given(r0, r1, k + 1)], axis=1)
        return raw - dots(mu[r0:r1, :], um[k * BLK:(k + 2) * BLK, :], ((1,), (1,)))

    def spans(start, size):
        return [(r, min(r + size, total)) for r in range(start, total, size)]

    for r0, r1 in spans(0, 2 * BLK):
        work[r0:r1, :] = pair_given(r0, r1, 0)
    part_ref[...] = jnp.zeros_like(part_ref)

    def step(k, carry):
        base = pl.multiple_of(k * BLK, BLK)
        flank = pl.ds(pl.multiple_of(lax.rem(k, 2) * BLK, BLK), BLK)
        inverse = invert_factor([work[pl.ds(base + g * GRP, GRP), flank] for g in range(BLK // GRP)])
        high_part, low_part = halves(jnp.concatenate(inverse, axis=0))
        wh[...] = high_part
        wl[...] = low_part

        for s in range(count):
            @pl.when(k == s)
            def _(s=s):
                lo, hi = s * BLK, s * BLK + BLK
                left = (s % 2) * BLK
                errands(s)
                for r0, r1 in spans(lo, 8 * BLK):
                    sh, sl = halves(work[r0:r1, left:left + BLK])
                    panel = mul2(sh, sl, wh[...], wl[...])
                    ph, pl_ = halves(panel)
                    high[r0:r1, lo:hi] = ph
                    low[r0:r1, lo:hi] = pl_
                    work[r0:r1, left:left + BLK] = panel
                x_ref[:, lo:hi] = work[order:order + x_ref.shape[0], left:left + BLK]

                @pl.when(jnp.logical_and(c == s, p >= s))
                def _():
                    block = work[pl.ds(pl.multiple_of(p * BLK, BLK), BLK), left:left + BLK]
                    r = lax.broadcasted_iota(jnp.int32, (BLK, BLK), 0)
                    l = lax.broadcasted_iota(jnp.int32, (BLK, BLK), 1)
                    part_ref[...] = jnp.where((p > s) | (r >= l), block, 0.0)

                if s % 2 == 0 and s + 1 < count:
                    for r0, r1 in spans(hi, 8 * BLK):
                        work[r0:r1, BLK:] = work[r0:r1, BLK:] - mul2(
                            high[r0:r1, lo:hi], low[r0:r1, lo:hi],
                            high[hi:hi + BLK, lo:hi], low[hi:hi + BLK, lo:hi])
                if s % 2 == 1 and s + 1 < count:
                    end = hi + 2 * BLK
                    for r0, r1 in spans(hi, 8 * BLK):
                        work[r0:r1, :] = pair_given(r0, r1, s + 1) - mul2(
                            high[r0:r1, :hi], low[r0:r1, :hi],
                            high[hi:end, :hi], low[hi:end, :hi])
        return carry

    lax.fori_loop(0, count, step, 0)

    stage_a(6)
    stage_b(6)
    stage_v(6)
    for first, later in spreads:
        for copy in first + later:
            copy.wait_send()
    for cuts, ring, mine in phases:
        for copy in ring:
            copy.wait_send()

    @pl.when(p == 0)
    def _():
        for cuts, ring, mine in phases:
            for copy in cuts:
                copy.wait_send()

    @pl.when(p == c)
    def _():
        for copy in vcuts:
            copy.wait_send()


def update_call(rank, left, right_factor, tiles, right, narrow):
    rows, cols = lax.axis_size("row"), lax.axis_size("col")
    depth, thin = cols // 2, BLK // rows
    extra, order = right.shape
    early = early_count(cols)
    late = (cols - early) // 2 + 1
    vm = pl.BlockSpec(memory_space=pltpu.VMEM)
    dma = pltpu.SemaphoreType.DMA
    wide, half = jnp.float32, jnp.bfloat16
    return pl.pallas_call(
        update_kernel,
        out_shape=(
            jax.ShapeDtypeStruct((2, cols, BLK, BLK), half),
            jax.ShapeDtypeStruct((rows, BLK, BLK), half),
            jax.ShapeDtypeStruct((narrow, order), wide),
            jax.ShapeDtypeStruct((BLK, BLK), wide),
        ),
        in_specs=[pl.BlockSpec(memory_space=pltpu.SMEM), vm, vm, pl.BlockSpec(memory_space=pl.ANY), vm],
        out_specs=(vm, vm, vm, vm),
        scratch_shapes=[
            pltpu.VMEM((2, BLK, BLK), half),
            pltpu.VMEM((BLK, order), wide),
            pltpu.VMEM((2, depth * (early + 1), BLK, BLK), wide),
            pltpu.VMEM((2, (depth - early // 2) * late, BLK, BLK), wide),
            pltpu.VMEM((early + 1, BLK, BLK), wide),
            pltpu.VMEM((late, BLK, BLK), wide),
            pltpu.VMEM((depth * (early + 1), thin, BLK), wide),
            pltpu.VMEM((depth * late, thin, BLK), wide),
            pltpu.VMEM((rows, BLK, BLK), half),
            pltpu.VMEM((order, BLK), half),
            pltpu.VMEM((order, BLK), half),
            pltpu.VMEM((order + extra, BLK), half),
            pltpu.VMEM((order + extra, order), half),
            pltpu.VMEM((order + extra, order), half),
            pltpu.VMEM((order + extra, 2 * BLK), wide),
            pltpu.VMEM((BLK, BLK), half),
            pltpu.VMEM((BLK, BLK), half),
            dma((2, depth)), dma((2, depth)), dma((2, depth)), dma((2, depth)),
            dma((2, rows)), dma((2,)), dma((2, depth)), dma((2, depth)),
            dma((2, 2, 20)), dma((2, 2, 20)), dma((2, 2, 16)), dma((2, 2, 16)),
            dma((rows,)), dma, dma((2, 20)), dma((2, 20)), dma((3,)),
        ],
        compiler_params=pltpu.CompilerParams(
            collective_id=0, has_side_effects=True, vmem_limit_bytes=56 * 2**20
        ),
        cost_estimate=pl.CostEstimate(flops=10**11, bytes_accessed=2 * 10**7, transcendentals=0),
    )(rank, left, right_factor, tiles, right)


def body(pan_left, pan_right, panel_rank, diag_tiles, col_right, column_rank):
    tile_rows = pan_left.shape[0]
    slab_rows = pan_left.shape[2]
    rank_width = pan_left.shape[3]
    tile_order = diag_tiles.shape[3]
    row_count = lax.axis_size("row")
    col_count = lax.axis_size("col")
    row_index = lax.axis_index("row")
    col_index = lax.axis_index("col")
    col_tiles = tile_rows * row_count // col_count
    narrow_rows = col_right.shape[2]
    rank_ids = lax.broadcasted_iota(jnp.int32, col_right.shape, 2) + col_index * narrow_rows
    tile_ids = lax.broadcasted_iota(jnp.int32, col_right.shape, 0) * row_count + row_index
    keep_right = (rank_ids < column_rank[:, :, None, None]) & (tile_ids >= 1)
    right_kept = jnp.where(keep_right, col_right, jnp.zeros_like(col_right))
    right_side = right_kept.astype(jnp.float32).reshape(-1, tile_order)
    count = right_side.shape[0]
    right_side = jnp.pad(right_side, ((0, -count % 16), (0, 0)))
    vu_all, vv_all, solved, lead_part = update_call(
        panel_rank, pan_left, pan_right, diag_tiles, right_side, count
    )
    flat_vu = vu_all.reshape(tile_rows, tile_order, 2 * rank_width)
    right_tiles, left_tiles = flat_vu[:, :, :rank_width], flat_vu[:, :, rank_width:]
    theirs = vv_all.reshape(tile_order, col_tiles, rank_width)
    own_gram = jnp.einsum(
        "anr,ans->ars", right_tiles, right_tiles, preferred_element_type=jnp.float32
    ).astype(jnp.bfloat16)
    products = jnp.einsum(
        "anr,ars->ans", left_tiles, own_gram, preferred_element_type=jnp.float32
    ).astype(jnp.bfloat16)
    product_rows = lax.dynamic_slice_in_dim(products, col_index * slab_rows, slab_rows, 1)
    correction = jnp.einsum(
        "ans,ams->anm", product_rows, left_tiles, preferred_element_type=jnp.float32
    )
    diag_new = diag_tiles - correction[:, None]
    cross_gram = jnp.einsum(
        "anr,nbs->abrs", right_tiles, theirs, preferred_element_type=jnp.float32
    ).astype(jnp.bfloat16)

    col_solved = solved.reshape(col_right.shape)

    tile_update = jnp.einsum(
        "anr,abrs->abns", left_tiles, cross_gram, preferred_element_type=jnp.float32
    )
    row_ids = lax.broadcasted_iota(jnp.int32, (tile_rows, col_tiles), 0) * row_count + row_index
    col_ids = lax.broadcasted_iota(jnp.int32, (tile_rows, col_tiles), 1) * col_count + col_index
    lower_mask = (row_ids > col_ids)[:, :, None, None]
    panel_update = jnp.where(lower_mask, tile_update, jnp.zeros_like(tile_update)).astype(
        jnp.bfloat16
    )
    panel_update = panel_update.reshape(tile_rows, 1, col_tiles, 1, tile_order, rank_width)
    return (panel_update, diag_new, lead_part, col_solved)


def solution(mesh):
    placed = (
        P(None, "row", "col", None),
        P(None, "row", "col", None),
        P(None, "row"),
        P(None, "row", "col", None),
        P(None, "row", "col", None),
        P(None, "row"),
    )
    return jax.shard_map(
        body,
        mesh=mesh,
        in_specs=placed,
        out_specs=(
            P(None, "row", None, "col", None, None),
            P(None, "row", "col", None),
            P("row", "col"),
            P(None, "row", "col", None),
        ),
        check_vma=False,
    )
```
